128 devices in a mesh: band: 16 (over z, y_hi, core), comp: 8 (over x, y_lo).
Axes of the slice: x: 4, y: 4 (y_hi: 2, y_lo: 2; y = y_hi * 2 + y_lo), z: 4, core: 2. Of those that a mesh axis runs over, the one named last changes fastest.
Arguments:
- tracer_mass: float32 [192, 8, 256, 512], P('comp', None, 'band'), may hold values from -6 to 6
- layer_mass: float32 [8, 256, 512], P('comp', 'band'), may hold values from 0.3 to 1.7
- zonal_wind: float32 [8, 256, 512], P('comp', 'band'), may hold values from -4 to 4
- merid_wind: float32 [8, 256, 512], P('comp', 'band'), may hold values from -4 to 4
- group_counts: int32 [8], replicated, may hold values from 1 to 24, 96 in all
- limiter_flags: int32 [96], replicated, may hold values 0 or 1
Outputs:
- tracers_out: float32 [192, 8, 256, 512], P('comp', None, 'band')
- height_out: float32 [8, 256, 512], P('comp', 'band')
- zonal_out: float32 [8, 256, 512], P('comp', 'band')
- merid_out: float32 [8, 256, 512], P('comp', 'band')
The draws below stay inside these ranges and needn't reach their ends.
Inputs may be any that keep to these rules, and one draw needn't show every extreme that they name: Group g lists the tracers numbered from the sum of the earlier groups' counts on, in its first group_counts[g] slots; the counts sum to 96 and the largest is exactly 24.
All inputs are finite; a program needn't handle non-finite values.
Results may differ from the reference program's by a relative error of at most 0.0003.
Values sent between devices are 32-bit elements; how exact they have to be, the bound alone decides.
A program may use at most 128 MiB of HBM per device.

```python
import math
import jax
import jax.numpy as jnp
import numpy as np
from jax import lax

L = 8
NX = 512
NTR = 96
SLOTS = 24
STEPS = 4
NY = 256
N_COMP = 8


def with_ends(entries, stream_key, least, high):
    longest = entries.shape.index(max(entries.shape))
    spots = []
    for shift in (0, 1):
        where = [jax.random.randint(jax.random.fold_in(stream_key, axis), (), 0, length) for axis, length in enumerate(entries.shape)]
        where[longest] = (where[longest] + shift) % entries.shape[longest]
        spots.append(tuple(where))
    return entries.at[spots[0]].set(least).at[spots[1]].set(high)


def block_scale(rng, dims, split, least, high):
    factor_of = 1.0
    for position, parts in split:
        draws = jax.random.uniform(jax.random.fold_in(jax.random.fold_in(rng, 6), position), (parts,), jnp.float32, least / len(split), high / len(split))
        factor_of = factor_of * jnp.repeat(jnp.exp(draws), dims[position] // parts).reshape((-1,) + (1,) * (len(dims) - 1 - position))
    return factor_of


def split_up(number_of, total, reach, lean):
    loads = [(1 << 20) // math.isqrt(rank ** lean) + 1 for rank in range(2, number_of + 1)]
    rest, given = total - reach - (number_of - 1), [1] * (number_of - 1)
    while rest > 0:
        free = [i for i in range(number_of - 1) if given[i] < reach]
        whole, budget = sum([loads[i] for i in free]), rest
        for i in free:
            extra = min(reach - given[i], max(1, budget * loads[i] // whole), rest)
            given[i] = given[i] + extra
            rest = rest - extra
    return np.array([reach] + given)


def ragged(key, count, total, limit, skew):
    if count == 2:
        one = jax.random.randint(key, (), max(1, total - limit), min(limit, total - 1) + 1)
        return jnp.stack([one, total - one])
    lengths = jnp.asarray(split_up(count, total, limit, skew), jnp.int32)
    pairs = (count - 1) // 2
    donor, sink = lengths[1:1 + 2 * pairs:2], lengths[2:2 + 2 * pairs:2]
    margin = jnp.minimum(donor - 1, limit - sink)
    passed = jax.random.randint(jax.random.fold_in(key, 1), (pairs,), 0, 1 << 20) % (margin + 1)
    lengths = lengths.at[1:1 + 2 * pairs:2].set(donor - passed).at[2:2 + 2 * pairs:2].set(sink + passed)
    return lengths[jax.random.permutation(jax.random.fold_in(key, 2), count)]


def gaussian(own_key, extent, deviation, limit, split=(), kind=jnp.bfloat16):
    drawn = deviation * jax.random.normal(own_key, extent, jnp.float32)
    if split:
        drawn = drawn * block_scale(own_key, extent, split, -0.22, 0.18)
    return jnp.clip(drawn, -limit, limit).astype(kind)


def setup_inputs(seed: int = 0) -> dict:
    key_list = jax.random.split(jax.random.key(seed), 7)
    tracer_mass = gaussian(key_list[0], (N_COMP * SLOTS, L, NY, NX), 1.0, 6.0, ((0, 8), (2, 16)), jnp.float32)
    layer_mass = jnp.clip(0.3 + 1.40000004 * jax.random.uniform(key_list[1], (L, NY, NX), jnp.float32) ** block_scale(key_list[1], (L, NY, NX), ((0, 8), (1, 16)), -0.2, 0.2), 0.3, 1.7)
    zonal_wind = gaussian(key_list[2], (L, NY, NX), 1.0, 4.0, ((0, 8), (1, 16)), jnp.float32)
    merid_wind = gaussian(key_list[3], (L, NY, NX), 1.0, 4.0, ((0, 8), (1, 16)), jnp.float32)
    group_counts = ragged(key_list[4], N_COMP, NTR, SLOTS, 2).astype(jnp.int32)
    limiter_flags = with_ends((jax.random.randint(key_list[5], (NTR,), 0, 2) < 1).astype(jnp.int32), jax.random.fold_in(key_list[5], 1), 0, 1)
    return dict(tracer_mass=tracer_mass, layer_mass=layer_mass, zonal_wind=zonal_wind, merid_wind=merid_wind, group_counts=group_counts, limiter_flags=limiter_flags)


time_step = 0.1
gravity = 0.25
coriolis = 0.5
mass_floor = 0.5


def face_value(left_out, left_in, right_in, right_out, limited):
    raw_face = (7.0 / 12.0) * (left_in + right_in) - (1.0 / 12.0) * (left_out + right_out)
    bounded = jnp.clip(raw_face, jnp.minimum(left_in, right_in), jnp.maximum(left_in, right_in))
    return jnp.where(limited > 0, bounded, raw_face)


def advance(height, zonal_now, merid_now, padded, first_row, total_rows):
    row_count = height.shape[1]
    pad_height, pad_merid, pad_geo = padded[0], padded[2], padded[3]
    flux_south = 0.25 * (pad_merid[:, :row_count + 1] + pad_merid[:, 1:]) * (pad_height[:, :row_count + 1] + pad_height[:, 1:])
    face_row = first_row + lax.broadcasted_iota(jnp.int32, flux_south.shape, 1)
    flux_south = jnp.where((face_row > 0) & (face_row < total_rows), flux_south, 0.0)
    flux_east = 0.25 * (zonal_now + jnp.roll(zonal_now, -1, 2)) * (height + jnp.roll(height, -1, 2))
    new_height = height - time_step * (flux_east - jnp.roll(flux_east, 1, 2) + flux_south[:, 1:] - flux_south[:, :row_count])
    geopot = pad_geo[:, 1:row_count + 1]
    slope_x = jnp.roll(geopot, -1, 2) - jnp.roll(geopot, 1, 2)
    slope_y = pad_geo[:, 2:] - pad_geo[:, :row_count]
    new_zonal = zonal_now + time_step * (coriolis * merid_now - 0.5 * slope_x)
    new_merid = merid_now - time_step * (coriolis * zonal_now + 0.5 * slope_y)
    return new_height, new_zonal, new_merid, flux_east, flux_south


def tracer_update(item_mass, padded_ratio, flux_east, flux_south, limited):
    row_count = item_mass.shape[1]
    mix_ratio = padded_ratio[:, 2:row_count + 2]
    east_face = face_value(jnp.roll(mix_ratio, 1, 2), mix_ratio, jnp.roll(mix_ratio, -1, 2), jnp.roll(mix_ratio, -2, 2), limited)
    east_term = flux_east * east_face
    south_face = face_value(padded_ratio[:, :row_count + 1], padded_ratio[:, 1:row_count + 2], padded_ratio[:, 2:row_count + 3], padded_ratio[:, 3:], limited)
    south_term = flux_south * south_face
    return item_mass - time_step * (east_term - jnp.roll(east_term, 1, 2) + south_term[:, 1:] - south_term[:, :row_count])


def reference(tracer_mass, layer_mass, zonal_wind, merid_wind, group_counts, limiter_flags):
    height, zonal_now, merid_now = layer_mass, zonal_wind, merid_wind
    total_rows = height.shape[1]
    heights, east_list, south_list = [], [], []
    for step_index in range(STEPS):
        geopot = gravity * jnp.cumsum(height[::-1], 0)[::-1]
        padded = jnp.pad(jnp.stack([height, zonal_now, merid_now, geopot]), ((0, 0), (0, 0), (1, 1), (0, 0)))
        stepped = advance(height, zonal_now, merid_now, padded, 0, total_rows)
        heights.append(height)
        east_list.append(stepped[3])
        south_list.append(stepped[4])
        height, zonal_now, merid_now = stepped[0], stepped[1], stepped[2]
    counts = group_counts.astype(jnp.int32)
    starts = (jnp.cumsum(counts) - counts).astype(jnp.int32)

    def one_slot(slot_index):
        group = slot_index // SLOTS
        within = slot_index % SLOTS
        tracer_id = jnp.minimum(starts[group] + within, NTR - 1)
        limited = limiter_flags[tracer_id]
        item_mass = tracer_mass[slot_index]
        for step_index in range(STEPS):
            mix_ratio = item_mass / jnp.maximum(heights[step_index], mass_floor)
            padded_ratio = jnp.pad(mix_ratio, ((0, 0), (2, 2), (0, 0)))
            item_mass = tracer_update(item_mass, padded_ratio, east_list[step_index], south_list[step_index], limited)
        return jnp.where(within < counts[group], item_mass, 0.0)

    tracers_out = lax.map(one_slot, jnp.arange(N_COMP * SLOTS, dtype=jnp.int32))
    return tracers_out, height, zonal_now, merid_now
```

```python
import functools

import jax
import jax.numpy as jnp
from jax import lax
from jax.experimental import pallas as pl
from jax.experimental.pallas import tpu as pltpu
from jax.sharding import PartitionSpec as P

STEPS = 4
CHUNK = 4
HALO = 8
ROWS = 16
EXT = ROWS + 2 * HALO
LEVELS = 8
NX = 512
SLOTS = 24
MESH_ID = pl.DeviceIdType.MESH
VMEM_LIMIT = 48 * 1024 * 1024

time_step = 0.1
gravity = 0.25
coriolis = 0.5
mass_floor = 0.5


def reach_of(step):
    return 2 * (STEPS - 1 - step)


def columns(i):
    return slice(128 * i, 128 * i + 128)


def level_rows(stage, first, stride):
    tiles = [
        stage[i, pl.ds(first, LEVELS, stride=stride), :] for i in range(NX // 128)
    ]
    return jnp.concatenate(tiles, axis=1)


def roll(value, shift):
    return pltpu.roll(value, shift % value.shape[-1], value.ndim - 1)


def gather_kernel(h_ref, u_ref, v_ref, out_ref, send_sem, recv_sem, halo_send, halo_recv):
    n_comp, n_band = lax.axis_size("comp"), lax.axis_size("band")
    level, band = lax.axis_index("comp"), lax.axis_index("band")
    has_low, has_high = band > 0, band < n_band - 1

    barrier = pltpu.get_barrier_semaphore()
    for p in range(1, n_comp):
        peer = lax.rem(level + p, n_comp)
        pl.semaphore_signal(barrier, inc=1, device_id={"comp": peer}, device_id_type=MESH_ID)

    @pl.when(has_low)
    def _():
        pl.semaphore_signal(barrier, inc=1, device_id={"band": band - 1}, device_id_type=MESH_ID)

    @pl.when(has_high)
    def _():
        pl.semaphore_signal(barrier, inc=1, device_id={"band": band + 1}, device_id_type=MESH_ID)

    for f, ref in enumerate((h_ref, u_ref, v_ref)):
        out_ref[level, f, HALO : HALO + ROWS, :] = ref[...]

    @pl.when(jnp.logical_not(has_low))
    def _():
        out_ref[level, :, 0:HALO, :] = jnp.zeros((3, HALO, NX), jnp.float32)

    @pl.when(jnp.logical_not(has_high))
    def _():
        out_ref[level, :, HALO + ROWS : EXT, :] = jnp.zeros((3, HALO, NX), jnp.float32)

    pl.semaphore_wait(
        barrier, n_comp - 1 + has_low.astype(jnp.int32) + has_high.astype(jnp.int32)
    )

    down = pltpu.make_async_remote_copy(
        src_ref=out_ref.at[level, :, pl.ds(HALO, HALO), :],
        dst_ref=out_ref.at[level, :, pl.ds(HALO + ROWS, HALO), :],
        send_sem=halo_send.at[0],
        recv_sem=halo_recv.at[0],
        device_id={"band": lax.max(band - 1, 0)},
        device_id_type=MESH_ID,
    )
    up = pltpu.make_async_remote_copy(
        src_ref=out_ref.at[level, :, pl.ds(ROWS, HALO), :],
        dst_ref=out_ref.at[level, :, pl.ds(0, HALO), :],
        send_sem=halo_send.at[1],
        recv_sem=halo_recv.at[1],
        device_id={"band": lax.min(band + 1, n_band - 1)},
        device_id_type=MESH_ID,
    )

    @pl.when(has_low)
    def _():
        down.start()

    @pl.when(has_high)
    def _():
        up.start()

    pieces = ((HALO, ROWS), (0, HALO), (HALO + ROWS, HALO))

    def copy(piece, p, owner):
        first, count = pieces[piece]
        return pltpu.make_async_remote_copy(
            src_ref=out_ref.at[owner, :, pl.ds(first, count), :],
            dst_ref=out_ref.at[owner, :, pl.ds(first, count), :],
            send_sem=send_sem.at[piece, p],
            recv_sem=recv_sem.at[piece, p],
            device_id={"comp": lax.rem(level + p, n_comp)},
            device_id_type=MESH_ID,
        )

    for p in range(1, n_comp):
        copy(0, p, level).start()

    @pl.when(has_low)
    def _():
        up.wait_recv()

    for p in range(1, n_comp):
        copy(1, p, level).start()

    @pl.when(has_high)
    def _():
        down.wait_recv()

    for p in range(1, n_comp):
        copy(2, p, level).start()

    @pl.when(has_low)
    def _():
        down.wait_send()

    @pl.when(has_high)
    def _():
        up.wait_send()

    for piece in range(3):
        for p in range(1, n_comp):
            copy(piece, p, level).wait_send()
            copy(piece, p, lax.rem(level + n_comp - p, n_comp)).wait_recv()


def gather_fields(height, zonal, merid):
    n_comp = lax.axis_size("comp")
    return pl.pallas_call(
        gather_kernel,
        out_shape=jax.ShapeDtypeStruct((n_comp, 3, EXT, NX), jnp.float32),
        in_specs=[pl.BlockSpec(memory_space=pltpu.VMEM)] * 3,
        out_specs=pl.BlockSpec(memory_space=pltpu.VMEM),
        scratch_shapes=[
            pltpu.SemaphoreType.DMA((3, n_comp)),
            pltpu.SemaphoreType.DMA((3, n_comp)),
            pltpu.SemaphoreType.DMA((2,)),
            pltpu.SemaphoreType.DMA((2,)),
        ],
        compiler_params=pltpu.CompilerParams(
            collective_id=0, has_side_effects=True, vmem_limit_bytes=16 * 1024 * 1024
        ),
    )(height, zonal, merid)


def dynamics_kernel(where_ref, g_ref, inv_ref, east_ref, south_ref, last_ref, h_buf, u_buf, v_buf, stage):
    first_row, level, total_rows = where_ref[0], where_ref[1], where_ref[2]
    stride = 3 * EXT

    for i in range(NX // 128):
        stage[i] = g_ref[:, columns(i)]

    @pl.loop(0, EXT)
    def _(j):
        for f, buf in enumerate((h_buf, u_buf, v_buf)):
            buf[j] = level_rows(stage, f * EXT + j, stride)

    depth = lax.broadcasted_iota(jnp.int32, (LEVELS, NX), 0)

    def geopot(h):
        total = h
        for gap in (1, 2, 4):
            moved = pltpu.roll(total, LEVELS - gap, 0)
            total = total + jnp.where(depth < LEVELS - gap, moved, 0.0)
        return gravity * total

    def south_flux(h_a, h_b, v_a, v_b, face):
        at = first_row + face - HALO
        inside = jnp.logical_and(at > 0, at < total_rows)
        scale = jnp.where(inside, 0.25 * time_step, 0.0)
        return scale * ((v_a + v_b) * (h_a + h_b))

    for step in range(STEPS):
        reach = reach_of(step)
        low, high = HALO - reach, HALO + ROWS + reach
        for j in (low - 2, low - 1, high, high + 1):
            inv_ref[step, j] = 1.0 / jnp.maximum(h_buf[j], mass_floor)
        h_before, h_here = h_buf[low - 1], h_buf[low]
        v_before, v_here = v_buf[low - 1], v_buf[low]
        south = south_flux(h_before, h_here, v_before, v_here, low)
        south_ref[step, low] = south

        def row(j, carry, step=step):
            h, v, geo_before, geo, south = carry
            h_after, v_after, u = h_buf[j + 1], v_buf[j + 1], u_buf[j]
            geo_after = geopot(h_after)
            south_after = south_flux(h, h_after, v, v_after, j + 1)
            east = (0.25 * time_step) * ((u + roll(u, -1)) * (h + roll(h, -1)))
            inv_ref[step, j] = 1.0 / jnp.maximum(h, mass_floor)
            east_ref[step, j] = east
            south_ref[step, j + 1] = south_after
            h_buf[j] = h - ((east - roll(east, 1)) + (south_after - south))
            u_buf[j] = u + time_step * (coriolis * v - 0.5 * (roll(geo, -1) - roll(geo, 1)))
            v_buf[j] = v - time_step * (coriolis * u + 0.5 * (geo_after - geo_before))
            return h_after, v_after, geo, geo_after, south_after

        lax.fori_loop(
            low, high, row, (h_here, v_here, geopot(h_before), geopot(h_here), south)
        )

    own = lax.broadcasted_iota(jnp.int32, (LEVELS, NX), 0) == level
    for f, buf in enumerate((h_buf, u_buf, v_buf)):
        for j in range(ROWS):
            picked = jnp.where(own, buf[HALO + j], 0.0)
            last_ref[f, pl.ds(j, 1), :] = jnp.sum(picked, axis=0, keepdims=True)


def dynamics(where, gathered):
    rows = jax.ShapeDtypeStruct((STEPS, EXT, LEVELS, NX), jnp.float32)
    vmem = pl.BlockSpec(memory_space=pltpu.VMEM)
    return pl.pallas_call(
        dynamics_kernel,
        out_shape=(rows, rows, rows, jax.ShapeDtypeStruct((3, ROWS, NX), jnp.float32)),
        in_specs=[pl.BlockSpec(memory_space=pltpu.SMEM), vmem],
        out_specs=(vmem,) * 4,
        scratch_shapes=[pltpu.VMEM((EXT, LEVELS, NX), jnp.float32)] * 3
        + [pltpu.VMEM((NX // 128, LEVELS * 3 * EXT, 128), jnp.float32)],
        compiler_params=pltpu.CompilerParams(vmem_limit_bytes=VMEM_LIMIT),
        cost_estimate=pl.CostEstimate(
            flops=10_000_000, bytes_accessed=8_000_000, transcendentals=0
        ),
    )(where, gathered)


def tracer_kernel(base, table_ref, m_ref, low_ref, high_ref, inv_ref, east_ref, south_ref, *rest):
    out_ref, buf, stage, low_stage, high_stage = rest[-5:]
    slot = base + pl.program_id(0)
    live = slot < table_ref[0]
    limited = table_ref[1 + slot] > 0

    def face(a_out, a, b, b_out, bounded):
        raw = (7.0 / 12.0) * (a + b) - (1.0 / 12.0) * (a_out + b_out)
        if not bounded:
            return raw
        return jnp.maximum(jnp.minimum(raw, jnp.maximum(a, b)), jnp.minimum(a, b))

    def advance(bounded):
        for step in range(STEPS):
            reach = reach_of(step)
            low, high = HALO - reach, HALO + ROWS + reach

            def ratio(j, step=step):
                return buf[j] * inv_ref[step, j]

            def row(j, carry, step=step):
                before, here, after, south = carry
                beyond = ratio(j + 2)
                south_after = south_ref[step, j + 1] * face(before, here, after, beyond, bounded)
                east = east_ref[step, j] * face(
                    roll(here, 1), here, roll(here, -1), roll(here, -2), bounded
                )
                new = buf[j] - ((east - roll(east, 1)) + (south_after - south))
                if step < STEPS - 1:
                    buf[j] = new
                else:
                    for i in range(NX // 128):
                        stage[i, pl.ds(j - HALO, LEVELS, stride=ROWS), :] = new[:, columns(i)]
                return here, after, beyond, south_after

            def rows(i, carry):
                for k in range(4):
                    carry = row(low + i * 4 + k, carry)
                return carry

            start = [ratio(low + k) for k in (-2, -1, 0, 1)]
            south = south_ref[step, low] * face(*start, bounded)
            lax.fori_loop(0, (high - low) // 4, rows, (*start[1:], south))

    @pl.when(live)
    def _():
        for i in range(NX // 128):
            stage[i] = m_ref[0, :, columns(i)]
            low_stage[i] = low_ref[0, :, columns(i)]
            high_stage[i] = high_ref[0, :, columns(i)]
        for j in range(HALO):
            buf[j] = level_rows(low_stage, j, HALO)
            buf[HALO + ROWS + j] = level_rows(high_stage, j, HALO)
        for j in range(ROWS):
            buf[HALO + j] = level_rows(stage, j, ROWS)

        @pl.when(limited)
        def _():
            advance(True)

        @pl.when(jnp.logical_not(limited))
        def _():
            advance(False)

        for i in range(NX // 128):
            out_ref[0, :, columns(i)] = stage[i]

    @pl.when(jnp.logical_not(live))
    def _():
        out_ref[...] = jnp.zeros_like(out_ref)


def tracer_chunk(base, count, table, mass, low, high, fluxes, so_far):
    slots = mass.shape[0]
    whole = pl.BlockSpec((STEPS, EXT, LEVELS, NX), lambda i, t: (0, 0, 0, 0), pipeline_mode=pl.Buffered(1))
    block = pl.BlockSpec((1, LEVELS * ROWS, NX), lambda i, t: (base + i, 0, 0))
    side = pl.BlockSpec((1, LEVELS * HALO, NX), lambda i, t: (i, 0, 0))
    operands = [table, mass, low, high, *fluxes]
    specs = [block, side, side, whole, whole, whole]
    aliases = {}
    if so_far is not None:
        aliases = {len(operands): 0}
        operands.append(so_far)
        specs.append(pl.BlockSpec(memory_space=pl.ANY))
    return pl.pallas_call(
        functools.partial(tracer_kernel, base),
        grid_spec=pltpu.PrefetchScalarGridSpec(
            num_scalar_prefetch=1,
            grid=(count,),
            in_specs=specs,
            out_specs=block,
            scratch_shapes=[
                pltpu.VMEM((EXT, LEVELS, NX), jnp.float32),
                pltpu.VMEM((NX // 128, LEVELS * ROWS, 128), jnp.float32),
                pltpu.VMEM((NX // 128, LEVELS * HALO, 128), jnp.float32),
                pltpu.VMEM((NX // 128, LEVELS * HALO, 128), jnp.float32),
            ],
        ),
        out_shape=jax.ShapeDtypeStruct((slots, LEVELS * ROWS, NX), jnp.float32),
        input_output_aliases=aliases,
        compiler_params=pltpu.CompilerParams(vmem_limit_bytes=VMEM_LIMIT),
        cost_estimate=pl.CostEstimate(
            flops=count * 11_000_000, bytes_accessed=6_000_000 + count * 800_000, transcendentals=0
        ),
    )(*operands)


def on_device(tracer_mass, layer_mass, zonal_wind, merid_wind, group_counts, limiter_flags):
    n_comp, n_band = lax.axis_size("comp"), lax.axis_size("band")
    comp, band = lax.axis_index("comp"), lax.axis_index("band")
    slots = tracer_mass.shape[0]

    groups = lax.broadcasted_iota(jnp.int32, (n_comp,), 0)
    count = jnp.sum(jnp.where(groups == comp, group_counts, 0))
    start = jnp.sum(jnp.where(groups < comp, group_counts, 0))
    numbers = lax.broadcasted_iota(jnp.int32, (slots, limiter_flags.shape[0]), 1)
    wanted = start + lax.broadcasted_iota(jnp.int32, (slots, limiter_flags.shape[0]), 0)
    flags = jnp.sum(jnp.where(numbers == wanted, limiter_flags[None, :], 0), 1)
    table = jnp.concatenate([count[None], flags])
    where = jnp.stack([band * ROWS, comp, n_band * ROWS]).astype(jnp.int32)

    forward = [(i, i + 1) for i in range(n_band - 1)]
    backward = [(i + 1, i) for i in range(n_band - 1)]

    gathered = gather_fields(
        layer_mass.reshape(ROWS, NX), zonal_wind.reshape(ROWS, NX), merid_wind.reshape(ROWS, NX)
    )
    lows, highs = [], []
    for base in range(0, slots, CHUNK):
        part = tracer_mass[base : base + CHUNK]
        lows.append(lax.ppermute(part[:, :, ROWS - HALO :], "band", forward))
        highs.append(lax.ppermute(part[:, :, :HALO], "band", backward))

    *fluxes, last = dynamics(where, gathered.reshape(n_comp * 3 * EXT, NX))
    mass = tracer_mass.reshape(slots, LEVELS * ROWS, NX)
    out = None
    for k, base in enumerate(range(0, slots, CHUNK)):
        low = lows[k].reshape(CHUNK, LEVELS * HALO, NX)
        high = highs[k].reshape(CHUNK, LEVELS * HALO, NX)
        out = tracer_chunk(base, CHUNK, table, mass, low, high, fluxes, out)
    tracers = out.reshape(tracer_mass.shape)
    return tracers, last[0][None], last[1][None], last[2][None]


def solution(mesh):
    placed = (
        P("comp", None, "band", None),
        P("comp", "band", None),
        P("comp", "band", None),
        P("comp", "band", None),
        P(),
        P(),
    )
    return jax.shard_map(
        on_device,
        mesh=mesh,
        in_specs=placed,
        out_specs=placed[:4],
        check_vma=False,
    )
```

```python
import functools

import jax
import jax.numpy as jnp
from jax import lax
from jax.experimental import pallas as pl
from jax.experimental.pallas import tpu as pltpu
from jax.sharding import PartitionSpec as P

STEPS = 4
CHUNK = 8
HALO = 8
ROWS = 16
EXT = ROWS + 2 * HALO
LEVELS = 8
NX = 512
SLOTS = 24
MESH_ID = pl.DeviceIdType.MESH
VMEM_LIMIT = 48 * 1024 * 1024

time_step = 0.1
gravity = 0.25
coriolis = 0.5
mass_floor = 0.5


def reach_of(step):
    return 2 * (STEPS - 1 - step)


def columns(i):
    return slice(128 * i, 128 * i + 128)


def level_rows(stage, first, stride):
    tiles = [
        stage[i, pl.ds(first, LEVELS, stride=stride), :] for i in range(NX // 128)
    ]
    return jnp.concatenate(tiles, axis=1)


def roll(value, shift):
    count = NX // 128
    tiles = [value[..., columns(i)] for i in range(count)]
    made = []
    for i in range(count):
        turns, at = divmod(i - shift, count)
        tile = tiles[at]
        if turns:
            tile = pltpu.roll(tile, (-turns) % 128, tile.ndim - 1)
        made.append(tile)
    return jnp.concatenate(made, axis=-1)


def dealing():
    source = lax.broadcasted_iota(jnp.int32, (NX, NX), 0)
    place = lax.broadcasted_iota(jnp.int32, (NX, NX), 1)
    deal = source == (place % 128) * (NX // 128) + place // 128
    return deal.astype(jnp.bfloat16)


def permuted(value, table):
    total = None
    rest = value
    for part in range(3):
        piece = rest.astype(jnp.bfloat16)
        moved = jnp.dot(piece, table, preferred_element_type=jnp.float32)
        total = moved if total is None else total + moved
        rest = rest - piece.astype(jnp.float32)
    return total


def gather_kernel(h_ref, u_ref, v_ref, deal_ref, out_ref, send_sem, recv_sem, halo_send, halo_recv):
    n_comp, n_band = lax.axis_size("comp"), lax.axis_size("band")
    level, band = lax.axis_index("comp"), lax.axis_index("band")
    has_low, has_high = band > 0, band < n_band - 1

    barrier = pltpu.get_barrier_semaphore()
    for p in range(1, n_comp):
        peer = lax.rem(level + p, n_comp)
        pl.semaphore_signal(barrier, inc=1, device_id={"comp": peer}, device_id_type=MESH_ID)

    @pl.when(has_low)
    def _():
        pl.semaphore_signal(barrier, inc=1, device_id={"band": band - 1}, device_id_type=MESH_ID)

    @pl.when(has_high)
    def _():
        pl.semaphore_signal(barrier, inc=1, device_id={"band": band + 1}, device_id_type=MESH_ID)

    for f, ref in enumerate((h_ref, u_ref, v_ref)):
        out_ref[level, f, HALO : HALO + ROWS, :] = permuted(ref[...], deal_ref[...])

    @pl.when(jnp.logical_not(has_low))
    def _():
        out_ref[level, :, 0:HALO, :] = jnp.zeros((3, HALO, NX), jnp.float32)

    @pl.when(jnp.logical_not(has_high))
    def _():
        out_ref[level, :, HALO + ROWS : EXT, :] = jnp.zeros((3, HALO, NX), jnp.float32)

    pl.semaphore_wait(
        barrier, n_comp - 1 + has_low.astype(jnp.int32) + has_high.astype(jnp.int32)
    )

    down = pltpu.make_async_remote_copy(
        src_ref=out_ref.at[level, :, pl.ds(HALO, HALO), :],
        dst_ref=out_ref.at[level, :, pl.ds(HALO + ROWS, HALO), :],
        send_sem=halo_send.at[0],
        recv_sem=halo_recv.at[0],
        device_id={"band": lax.max(band - 1, 0)},
        device_id_type=MESH_ID,
    )
    up = pltpu.make_async_remote_copy(
        src_ref=out_ref.at[level, :, pl.ds(ROWS, HALO), :],
        dst_ref=out_ref.at[level, :, pl.ds(0, HALO), :],
        send_sem=halo_send.at[1],
        recv_sem=halo_recv.at[1],
        device_id={"band": lax.min(band + 1, n_band - 1)},
        device_id_type=MESH_ID,
    )

    @pl.when(has_low)
    def _():
        down.start()

    @pl.when(has_high)
    def _():
        up.start()

    pieces = ((HALO, ROWS), (0, HALO), (HALO + ROWS, HALO))

    def copy(piece, p, owner):
        first, count = pieces[piece]
        return pltpu.make_async_remote_copy(
            src_ref=out_ref.at[owner, :, pl.ds(first, count), :],
            dst_ref=out_ref.at[owner, :, pl.ds(first, count), :],
            send_sem=send_sem.at[piece, p],
            recv_sem=recv_sem.at[piece, p],
            device_id={"comp": lax.rem(level + p, n_comp)},
            device_id_type=MESH_ID,
        )

    for p in range(1, n_comp):
        copy(0, p, level).start()

    @pl.when(has_low)
    def _():
        up.wait_recv()

    for p in range(1, n_comp):
        copy(1, p, level).start()

    @pl.when(has_high)
    def _():
        down.wait_recv()

    for p in range(1, n_comp):
        copy(2, p, level).start()

    @pl.when(has_low)
    def _():
        down.wait_send()

    @pl.when(has_high)
    def _():
        up.wait_send()

    for piece in range(3):
        for p in range(1, n_comp):
            copy(piece, p, level).wait_send()
            copy(piece, p, lax.rem(level + n_comp - p, n_comp)).wait_recv()


def gather_fields(height, zonal, merid, deal):
    n_comp = lax.axis_size("comp")
    return pl.pallas_call(
        gather_kernel,
        out_shape=jax.ShapeDtypeStruct((n_comp, 3, EXT, NX), jnp.float32),
        in_specs=[pl.BlockSpec(memory_space=pltpu.VMEM)] * 4,
        out_specs=pl.BlockSpec(memory_space=pltpu.VMEM),
        scratch_shapes=[
            pltpu.SemaphoreType.DMA((3, n_comp)),
            pltpu.SemaphoreType.DMA((3, n_comp)),
            pltpu.SemaphoreType.DMA((2,)),
            pltpu.SemaphoreType.DMA((2,)),
        ],
        compiler_params=pltpu.CompilerParams(
            collective_id=0, has_side_effects=True, vmem_limit_bytes=16 * 1024 * 1024
        ),
    )(height, zonal, merid, deal)


def dynamics_kernel(where_ref, g_ref, back_ref, inv_ref, east_ref, south_ref, last_ref, h_buf, u_buf, v_buf, stage, picked_ref):
    first_row, level, total_rows = where_ref[0], where_ref[1], where_ref[2]
    stride = 3 * EXT

    for i in range(NX // 128):
        stage[i] = g_ref[:, columns(i)]

    @pl.loop(0, EXT)
    def _(j):
        for f, buf in enumerate((h_buf, u_buf, v_buf)):
            buf[j] = level_rows(stage, f * EXT + j, stride)

    depth = lax.broadcasted_iota(jnp.int32, (LEVELS, NX), 0)

    def geopot(h):
        total = h
        for gap in (1, 2, 4):
            moved = pltpu.roll(total, LEVELS - gap, 0)
            total = total + jnp.where(depth < LEVELS - gap, moved, 0.0)
        return gravity * total

    def south_flux(h_a, h_b, v_a, v_b, face):
        at = first_row + face - HALO
        inside = jnp.logical_and(at > 0, at < total_rows)
        scale = jnp.where(inside, 0.25 * time_step, 0.0)
        return scale * ((v_a + v_b) * (h_a + h_b))

    for step in range(STEPS):
        reach = reach_of(step)
        low, high = HALO - reach, HALO + ROWS + reach
        for j in (low - 2, low - 1, high, high + 1):
            inv_ref[step, j] = 1.0 / jnp.maximum(h_buf[j], mass_floor)
        h_before, h_here = h_buf[low - 1], h_buf[low]
        v_before, v_here = v_buf[low - 1], v_buf[low]
        south = south_flux(h_before, h_here, v_before, v_here, low)
        south_ref[step, low] = south

        def row(j, carry, step=step):
            h, v, geo_before, geo, south = carry
            h_after, v_after, u = h_buf[j + 1], v_buf[j + 1], u_buf[j]
            geo_after = geopot(h_after)
            south_after = south_flux(h, h_after, v, v_after, j + 1)
            east = (0.25 * time_step) * ((u + roll(u, -1)) * (h + roll(h, -1)))
            inv_ref[step, j] = 1.0 / jnp.maximum(h, mass_floor)
            east_ref[step, j] = east
            south_ref[step, j + 1] = south_after
            h_buf[j] = h - ((east - roll(east, 1)) + (south_after - south))
            u_buf[j] = u + time_step * (coriolis * v - 0.5 * (roll(geo, -1) - roll(geo, 1)))
            v_buf[j] = v - time_step * (coriolis * u + 0.5 * (geo_after - geo_before))
            return h_after, v_after, geo, geo_after, south_after

        carry = (h_here, v_here, geopot(h_before), geopot(h_here), south)
        for j in range(low, high):
            carry = row(j, carry)

    own = lax.broadcasted_iota(jnp.int32, (LEVELS, NX), 0) == level
    for f, buf in enumerate((h_buf, u_buf, v_buf)):
        for j in range(ROWS):
            picked = jnp.where(own, buf[HALO + j], 0.0)
            picked_ref[pl.ds(f * ROWS + j, 1), :] = jnp.sum(picked, axis=0, keepdims=True)
    last_ref[...] = permuted(picked_ref[...], back_ref[...])


def dynamics(where, gathered, back):
    rows = jax.ShapeDtypeStruct((STEPS, EXT, LEVELS, NX), jnp.float32)
    vmem = pl.BlockSpec(memory_space=pltpu.VMEM)
    return pl.pallas_call(
        dynamics_kernel,
        out_shape=(rows, rows, rows, jax.ShapeDtypeStruct((3 * ROWS, NX), jnp.float32)),
        in_specs=[pl.BlockSpec(memory_space=pltpu.SMEM), vmem, vmem],
        out_specs=(vmem,) * 4,
        scratch_shapes=[pltpu.VMEM((EXT, LEVELS, NX), jnp.float32)] * 3
        + [
            pltpu.VMEM((NX // 128, LEVELS * 3 * EXT, 128), jnp.float32),
            pltpu.VMEM((3 * ROWS, NX), jnp.float32),
        ],
        compiler_params=pltpu.CompilerParams(vmem_limit_bytes=VMEM_LIMIT),
        cost_estimate=pl.CostEstimate(
            flops=10_000_000, bytes_accessed=8_000_000, transcendentals=0
        ),
    )(where, gathered, back)


def tracer_kernel(
    base, table_ref, m_ref, low_ref, high_ref, deal_ref, back_ref, inv_ref, east_ref, south_ref, *rest
):
    out_ref, buf, stage, low_stage, high_stage = rest[-5:]
    slot = base + pl.program_id(0)
    live = slot < table_ref[0]
    limited = table_ref[1 + slot] > 0
    tiles = NX // 128

    def face(a_out, a, b, b_out):
        raw = (7.0 / 12.0) * (a + b) - (1.0 / 12.0) * (a_out + b_out)
        bounded = jnp.maximum(jnp.minimum(raw, jnp.maximum(a, b)), jnp.minimum(a, b))
        return jnp.where(limited, bounded, raw)

    def advance():
        for step in range(STEPS):
            reach = reach_of(step)
            low, high = HALO - reach, HALO + ROWS + reach

            def ratio(j, step=step):
                return buf[j] * inv_ref[step, j]

            before, here, after = ratio(low - 1), ratio(low), ratio(low + 1)
            south = south_ref[step, low] * face(ratio(low - 2), before, here, after)
            for j in range(low, high):
                beyond = ratio(j + 2)
                south_after = south_ref[step, j + 1] * face(before, here, after, beyond)
                east = east_ref[step, j] * face(roll(here, 1), here, roll(here, -1), roll(here, -2))
                new = buf[j] - ((east - roll(east, 1)) + (south_after - south))
                if step < STEPS - 1:
                    buf[j] = new
                else:
                    for i in range(tiles):
                        stage[i, pl.ds(j - HALO, LEVELS, stride=ROWS), :] = new[:, columns(i)]
                before, here, after, south = here, after, beyond, south_after

    @pl.when(live)
    def _():
        for ref, to in ((m_ref, stage), (low_ref, low_stage), (high_ref, high_stage)):
            dealt = permuted(ref[0], deal_ref[...])
            for i in range(tiles):
                to[i] = dealt[:, columns(i)]
        for j in range(HALO):
            buf[j] = level_rows(low_stage, j, HALO)
            buf[HALO + ROWS + j] = level_rows(high_stage, j, HALO)
        for j in range(ROWS):
            buf[HALO + j] = level_rows(stage, j, ROWS)
        advance()
        final = jnp.concatenate([stage[i] for i in range(tiles)], axis=1)
        out_ref[0] = permuted(final, back_ref[...])

    @pl.when(jnp.logical_not(live))
    def _():
        out_ref[...] = jnp.zeros_like(out_ref)


def tracer_chunk(base, count, table, mass, low, high, tables, fluxes, so_far):
    slots = mass.shape[0]
    whole = pl.BlockSpec((STEPS, EXT, LEVELS, NX), lambda i, t: (0, 0, 0, 0), pipeline_mode=pl.Buffered(1))
    block = pl.BlockSpec((1, LEVELS * ROWS, NX), lambda i, t: (base + i, 0, 0))
    side = pl.BlockSpec((1, LEVELS * HALO, NX), lambda i, t: (i, 0, 0))
    square = pl.BlockSpec((NX, NX), lambda i, t: (0, 0), pipeline_mode=pl.Buffered(1))
    operands = [table, mass, low, high, *tables, *fluxes]
    specs = [block, side, side, square, square, whole, whole, whole]
    aliases = {}
    if so_far is not None:
        aliases = {len(operands): 0}
        operands.append(so_far)
        specs.append(pl.BlockSpec(memory_space=pl.ANY))
    return pl.pallas_call(
        functools.partial(tracer_kernel, base),
        grid_spec=pltpu.PrefetchScalarGridSpec(
            num_scalar_prefetch=1,
            grid=(count,),
            in_specs=specs,
            out_specs=block,
            scratch_shapes=[
                pltpu.VMEM((EXT, LEVELS, NX), jnp.float32),
                pltpu.VMEM((NX // 128, LEVELS * ROWS, 128), jnp.float32),
                pltpu.VMEM((NX // 128, LEVELS * HALO, 128), jnp.float32),
                pltpu.VMEM((NX // 128, LEVELS * HALO, 128), jnp.float32),
            ],
        ),
        out_shape=jax.ShapeDtypeStruct((slots, LEVELS * ROWS, NX), jnp.float32),
        input_output_aliases=aliases,
        compiler_params=pltpu.CompilerParams(vmem_limit_bytes=VMEM_LIMIT),
        cost_estimate=pl.CostEstimate(
            flops=count * 11_000_000, bytes_accessed=6_000_000 + count * 800_000, transcendentals=0
        ),
    )(*operands)


def on_device(tracer_mass, layer_mass, zonal_wind, merid_wind, group_counts, limiter_flags):
    n_comp, n_band = lax.axis_size("comp"), lax.axis_size("band")
    comp, band = lax.axis_index("comp"), lax.axis_index("band")
    slots = tracer_mass.shape[0]

    groups = lax.broadcasted_iota(jnp.int32, (n_comp,), 0)
    count = jnp.sum(jnp.where(groups == comp, group_counts, 0))
    start = jnp.sum(jnp.where(groups < comp, group_counts, 0))
    numbers = lax.broadcasted_iota(jnp.int32, (slots, limiter_flags.shape[0]), 1)
    wanted = start + lax.broadcasted_iota(jnp.int32, (slots, limiter_flags.shape[0]), 0)
    flags = jnp.sum(jnp.where(numbers == wanted, limiter_flags[None, :], 0), 1)
    table = jnp.concatenate([count[None], flags])
    where = jnp.stack([band * ROWS, comp, n_band * ROWS]).astype(jnp.int32)

    forward = [(i, i + 1) for i in range(n_band - 1)]
    backward = [(i + 1, i) for i in range(n_band - 1)]

    deal = dealing()
    back = deal.T
    gathered = gather_fields(
        layer_mass.reshape(ROWS, NX), zonal_wind.reshape(ROWS, NX), merid_wind.reshape(ROWS, NX), deal
    )
    mass, gathered = lax.optimization_barrier((tracer_mass, gathered))
    lows, highs = [], []
    for base in range(0, slots, CHUNK):
        part = mass[base : base + CHUNK]
        lows.append(lax.ppermute(part[:, :, ROWS - HALO :], "band", forward))
        highs.append(lax.ppermute(part[:, :, :HALO], "band", backward))

    *fluxes, last = dynamics(where, gathered.reshape(n_comp * 3 * EXT, NX), back)
    mass = tracer_mass.reshape(slots, LEVELS * ROWS, NX)
    out = None
    for k, base in enumerate(range(0, slots, CHUNK)):
        low = lows[k].reshape(CHUNK, LEVELS * HALO, NX)
        high = highs[k].reshape(CHUNK, LEVELS * HALO, NX)
        out = tracer_chunk(base, CHUNK, table, mass, low, high, (deal, back), fluxes, out)
    tracers = out.reshape(tracer_mass.shape)
    last = last.reshape(3, 1, ROWS, NX)
    return tracers, last[0], last[1], last[2]


def solution(mesh):
    placed = (
        P("comp", None, "band", None),
        P("comp", "band", None),
        P("comp", "band", None),
        P("comp", "band", None),
        P(),
        P(),
    )
    return jax.shard_map(
        on_device,
        mesh=mesh,
        in_specs=placed,
        out_specs=placed[:4],
        check_vma=False,
    )
```

```python
import jax
import jax.numpy as jnp
from jax import lax
from jax.experimental import pallas as pl
from jax.experimental.pallas import tpu as pltpu
from jax.sharding import PartitionSpec as P

STEPS = 4
HALO = 8
ROWS = 16
EXT = ROWS + 2 * HALO
LEVELS = 8
NX = 512
SLOTS = 24
BLOCK = 4
EARLY = 4
TILES = NX // 128
MESH_ID = pl.DeviceIdType.MESH
VMEM_LIMIT = 48 * 1024 * 1024

time_step = 0.1
gravity = 0.25
coriolis = 0.5
mass_floor = 0.5


def reach_of(step):
    return 2 * (STEPS - 1 - step)


def columns(i):
    return slice(128 * i, 128 * i + 128)


def level_rows(stage, first, stride):
    tiles = [
        stage[i, pl.ds(first, LEVELS, stride=stride), :] for i in range(NX // 128)
    ]
    return jnp.concatenate(tiles, axis=1)


def roll(value, shift):
    count = NX // 128
    tiles = [value[..., columns(i)] for i in range(count)]
    made = []
    for i in range(count):
        turns, at = divmod(i - shift, count)
        tile = tiles[at]
        if turns and tile.ndim == 3:
            turned = [pltpu.roll(tile[k], (-turns) % 128, 1) for k in range(tile.shape[0])]
            tile = jnp.stack(turned)
        elif turns:
            tile = pltpu.roll(tile, (-turns) % 128, 1)
        made.append(tile)
    return jnp.concatenate(made, axis=-1)


def dealing():
    source = lax.broadcasted_iota(jnp.int32, (NX, NX), 0)
    place = lax.broadcasted_iota(jnp.int32, (NX, NX), 1)
    deal = source == (place % 128) * (NX // 128) + place // 128
    return deal.astype(jnp.bfloat16)


def permuted(value, table):
    total = None
    rest = value
    for part in range(3):
        piece = rest.astype(jnp.bfloat16)
        moved = jnp.dot(piece, table, preferred_element_type=jnp.float32)
        total = moved if total is None else total + moved
        rest = rest - piece.astype(jnp.float32)
    return total


def dynamics(fields, back_ref, inv_ref, east_ref, south_ref, last_refs, h_buf, u_buf, v_buf, stage, picked_ref):
    level, band = lax.axis_index("comp"), lax.axis_index("band")
    first_row, total_rows = band * ROWS, lax.axis_size("band") * ROWS
    stride = 3 * EXT

    for k in range(LEVELS):
        for f in range(3):
            rows = slice((k * 3 + f) * EXT, (k * 3 + f + 1) * EXT)
            for i in range(TILES):
                stage[i, rows, :] = fields[k, f, :, columns(i)]

    @pl.loop(0, EXT)
    def _(j):
        for f, buf in enumerate((h_buf, u_buf, v_buf)):
            buf[j] = level_rows(stage, f * EXT + j, stride)

    depth = lax.broadcasted_iota(jnp.int32, (LEVELS, NX), 0)

    def geopot(h):
        total = h
        for gap in (1, 2, 4):
            moved = pltpu.roll(total, LEVELS - gap, 0)
            total = total + jnp.where(depth < LEVELS - gap, moved, 0.0)
        return gravity * total

    def south_flux(h_a, h_b, v_a, v_b, face):
        at = first_row + face - HALO
        inside = jnp.logical_and(at > 0, at < total_rows)
        scale = jnp.where(inside, 0.25 * time_step, 0.0)
        return scale * ((v_a + v_b) * (h_a + h_b))

    for step in range(STEPS):
        reach = reach_of(step)
        low, high = HALO - reach, HALO + ROWS + reach
        for j in (low - 2, low - 1, high, high + 1):
            inv_ref[step, j] = 1.0 / jnp.maximum(h_buf[j], mass_floor)
        h_before, h_here = h_buf[low - 1], h_buf[low]
        v_before, v_here = v_buf[low - 1], v_buf[low]
        south = south_flux(h_before, h_here, v_before, v_here, low)
        south_ref[step, low] = south

        def row(j, carry, step=step):
            h, v, geo_before, geo, south = carry
            h_after, v_after, u = h_buf[j + 1], v_buf[j + 1], u_buf[j]
            geo_after = geopot(h_after)
            south_after = south_flux(h, h_after, v, v_after, j + 1)
            east = (0.25 * time_step) * ((u + roll(u, -1)) * (h + roll(h, -1)))
            inv_ref[step, j] = 1.0 / jnp.maximum(h, mass_floor)
            east_ref[step, j] = east
            south_ref[step, j + 1] = south_after
            h_buf[j] = h - ((east - roll(east, 1)) + (south_after - south))
            u_buf[j] = u + time_step * (coriolis * v - 0.5 * (roll(geo, -1) - roll(geo, 1)))
            v_buf[j] = v - time_step * (coriolis * u + 0.5 * (geo_after - geo_before))
            return h_after, v_after, geo, geo_after, south_after

        carry = (h_here, v_here, geopot(h_before), geopot(h_here), south)
        for j in range(low, high):
            carry = row(j, carry)

    own = lax.broadcasted_iota(jnp.int32, (LEVELS, NX), 0) == level
    for f, buf in enumerate((h_buf, u_buf, v_buf)):
        for j in range(ROWS):
            picked = jnp.where(own, buf[HALO + j], 0.0)
            picked_ref[pl.ds(f * ROWS + j, 1), :] = jnp.sum(picked, axis=0, keepdims=True)
    last = permuted(picked_ref[...], back_ref[...])
    for f in range(3):
        last_refs[f][...] = last[f * ROWS : (f + 1) * ROWS]


def advance_slot(limited, buf, stage, inv_ref, east_ref, south_ref):
    def face(a_out, a, b, b_out):
        raw = (7.0 / 12.0) * (a + b) - (1.0 / 12.0) * (a_out + b_out)
        bounded = jnp.maximum(jnp.minimum(raw, jnp.maximum(a, b)), jnp.minimum(a, b))
        return jnp.where(limited, bounded, raw)

    for step in range(STEPS):
        reach = reach_of(step)
        low, high = HALO - reach, HALO + ROWS + reach

        def ratios(j, n, step=step):
            return buf[j : j + n] * inv_ref[step, j : j + n]

        r = ratios(low - 2, 4)
        south = south_ref[step, low : low + 1] * face(r[0:1], r[1:2], r[2:3], r[3:4])
        r = r[1:]
        for j in range(low, high, BLOCK):
            r = jnp.concatenate([r, ratios(j + 2, BLOCK)], axis=0)
            here = r[1 : BLOCK + 1]
            after = south_ref[step, j + 1 : j + 1 + BLOCK] * face(
                r[0:BLOCK], here, r[2 : BLOCK + 2], r[3 : BLOCK + 3]
            )
            south = jnp.concatenate([south, after], axis=0)
            east = east_ref[step, j : j + BLOCK] * face(
                roll(here, 1), here, roll(here, -1), roll(here, -2)
            )
            new = buf[j : j + BLOCK] - ((east - roll(east, 1)) + (after - south[:BLOCK]))
            if step < STEPS - 1:
                buf[j : j + BLOCK] = new
            else:
                for k in range(BLOCK):
                    for i in range(TILES):
                        place = pl.ds(j + k - HALO, LEVELS, stride=ROWS)
                        stage[i, place, :] = new[k][:, columns(i)]
            r, south = r[BLOCK:], south[BLOCK:]


def kernel(
    table_ref, h_ref, u_ref, v_ref, deal_ref, back_ref, mass_ref,
    out_ref, h_out, u_out, v_out,
    fields, masses, lows, highs, inv_ref, east_ref, south_ref,
    h_buf, u_buf, v_buf, g_stage, picked_ref, buf, stage, low_stage, high_stage,
    load_sem, store_sem, rows_send, rows_recv, side_send, side_recv,
    field_send, field_recv, swap_sem,
):
    n_comp, n_band = lax.axis_size("comp"), lax.axis_size("band")
    level, band = lax.axis_index("comp"), lax.axis_index("band")
    core = lax.rem(band, 2)
    beside = level + 1 - 2 * lax.rem(level, 2)
    sibling = band + 1 - 2 * core
    has_low, has_high = band > 0, band < n_band - 1
    outer = lax.rem(band + n_band - 1 + 2 * core, n_band)
    has_outer = jnp.logical_and(band > 0, band < n_band - 1)
    slots = masses.shape[0]

    def load(t):
        return pltpu.make_async_copy(mass_ref.at[t], masses.at[t], load_sem.at[t])

    def store(t):
        return pltpu.make_async_copy(masses.at[t], out_ref.at[t], store_sem.at[t])

    def down(t):
        return pltpu.make_async_remote_copy(
            src_ref=mass_ref.at[t, :, pl.ds(0, HALO), :],
            dst_ref=highs.at[t],
            send_sem=rows_send.at[0, t],
            recv_sem=rows_recv.at[0, t],
            device_id={"band": lax.max(band - 1, 0)},
            device_id_type=MESH_ID,
        )

    def up(t):
        return pltpu.make_async_remote_copy(
            src_ref=mass_ref.at[t, :, pl.ds(HALO, HALO), :],
            dst_ref=lows.at[t],
            send_sem=rows_send.at[1, t],
            recv_sem=rows_recv.at[1, t],
            device_id={"band": lax.min(band + 1, n_band - 1)},
            device_id_type=MESH_ID,
        )

    def send_rows(first, last):
        @pl.when(has_low)
        def _():
            @pl.loop(first, last)
            def _(t):
                down(t).start()

        @pl.when(has_high)
        def _():
            @pl.loop(first, last)
            def _(t):
                up(t).start()

    barrier = pltpu.get_barrier_semaphore()
    peers = [{"comp": beside}, {"band": sibling}]
    peers += [{"comp": lax.rem(level + 2 * p, n_comp)} for p in range(1, n_comp // 2)]
    for peer in peers:
        pl.semaphore_signal(barrier, inc=1, device_id=peer, device_id_type=MESH_ID)

    @pl.when(has_outer)
    def _():
        pl.semaphore_signal(barrier, inc=1, device_id={"band": outer}, device_id_type=MESH_ID)

    @pl.loop(0, slots)
    def _(t):
        load(t).start()

    own = jnp.concatenate([h_ref[...], u_ref[...], v_ref[...]], axis=0)
    own = permuted(own, deal_ref[...])
    for f in range(3):
        fields[level, f, HALO : HALO + ROWS, :] = own[f * ROWS : (f + 1) * ROWS]

    edge = pl.multiple_of(2 * (HALO + HALO // 2) * core, HALO)

    @pl.when(jnp.logical_not(has_outer))
    def _():
        fields[level, :, pl.ds(edge, HALO), :] = jnp.zeros((3, HALO, NX), jnp.float32)

    @pl.when(jnp.logical_not(has_low))
    def _():
        lows[...] = jnp.zeros_like(lows)

    @pl.when(jnp.logical_not(has_high))
    def _():
        highs[...] = jnp.zeros_like(highs)

    pl.semaphore_wait(barrier, len(peers) + has_outer.astype(jnp.int32))

    side = pltpu.make_async_remote_copy(
        src_ref=fields.at[level, :, pl.ds(pl.multiple_of(HALO + HALO * core, HALO), HALO), :],
        dst_ref=fields.at[level, :, pl.ds(pl.multiple_of(3 * HALO * (1 - core), HALO), HALO), :],
        send_sem=side_send,
        recv_sem=side_recv,
        device_id={"band": outer},
        device_id_type=MESH_ID,
    )

    @pl.when(has_outer)
    def _():
        side.start()

    def piece(k, owner, target, lane):
        rows = pl.ds(HALO, ROWS) if k == 0 else pl.ds(edge, HALO)
        return pltpu.make_async_remote_copy(
            src_ref=fields.at[owner, :, rows, :],
            dst_ref=fields.at[owner, :, rows, :],
            send_sem=field_send.at[k, lane],
            recv_sem=field_recv.at[k, lane],
            device_id={"comp": target},
            device_id_type=MESH_ID,
        )

    ring = range(1, n_comp // 2)

    def to_all(k):
        sends = [piece(k, level, beside, 0)]
        sends += [piece(k, level, lax.rem(level + 2 * p, n_comp), p) for p in ring]
        return sends

    def passed_on(k):
        return [piece(k, beside, lax.rem(level + 2 * p, n_comp), n_comp // 2 + p) for p in ring]

    def arriving(k):
        far = [lax.rem(level + n_comp - 2 * p, n_comp) for p in ring]
        waits = [piece(k, owner, beside, p) for p, owner in zip(ring, far)]
        far = [lax.rem(beside + n_comp - 2 * p, n_comp) for p in ring]
        return waits + [piece(k, owner, beside, n_comp // 2 + p) for p, owner in zip(ring, far)]

    for send in to_all(0):
        send.start()
    send_rows(0, EARLY)

    @pl.when(has_outer)
    def _():
        side.wait_recv()

    for send in to_all(1):
        send.start()
    for k in range(2):
        piece(k, beside, beside, 0).wait_recv()
        for send in passed_on(k):
            send.start()
    for wait in arriving(0):
        wait.wait_recv()

    swap = pltpu.make_async_remote_copy(
        src_ref=fields.at[:, :, pl.ds(pl.multiple_of(2 * HALO - HALO * core, HALO), HALO), :],
        dst_ref=fields.at[:, :, pl.ds(pl.multiple_of(3 * HALO * core, HALO), HALO), :],
        send_sem=swap_sem.at[0],
        recv_sem=swap_sem.at[1],
        device_id={"band": sibling},
        device_id_type=MESH_ID,
    )
    swap.start()
    for wait in arriving(1):
        wait.wait_recv()
    send_rows(EARLY, slots)
    swap.wait_recv()

    dynamics(
        fields, back_ref, inv_ref, east_ref, south_ref, (h_out, u_out, v_out),
        h_buf, u_buf, v_buf, g_stage, picked_ref,
    )

    @pl.loop(0, slots)
    def _(t):
        load(t).wait()

        @pl.when(has_low)
        def _():
            up(t).wait_recv()

        @pl.when(has_high)
        def _():
            down(t).wait_recv()

        sides = (LEVELS * HALO, NX)
        blocks = (
            (masses[t].reshape(LEVELS * ROWS, NX), stage),
            (lows[t].reshape(sides), low_stage),
            (highs[t].reshape(sides), high_stage),
        )
        for block, to in blocks:
            dealt = permuted(block, deal_ref[...])
            for i in range(TILES):
                to[i] = dealt[:, columns(i)]
        for j in range(HALO):
            buf[j] = level_rows(low_stage, j, HALO)
            buf[HALO + ROWS + j] = level_rows(high_stage, j, HALO)
        for j in range(ROWS):
            buf[HALO + j] = level_rows(stage, j, ROWS)
        advance_slot(table_ref[1 + t] > 0, buf, stage, inv_ref, east_ref, south_ref)
        final = jnp.concatenate([stage[i] for i in range(TILES)], axis=1)
        final = permuted(final, back_ref[...])
        final = jnp.where(t < table_ref[0], final, 0.0)
        masses[t] = final.reshape(LEVELS, ROWS, NX)
        store(t).start()

    @pl.loop(0, slots)
    def _(t):
        store(t).wait()

        @pl.when(has_low)
        def _():
            down(t).wait_send()

        @pl.when(has_high)
        def _():
            up(t).wait_send()

    @pl.when(has_outer)
    def _():
        side.wait_send()

    swap.wait_send()
    for k in range(2):
        for send in to_all(k) + passed_on(k):
            send.wait_send()


def on_device(tracer_mass, layer_mass, zonal_wind, merid_wind, group_counts, limiter_flags):
    n_comp = lax.axis_size("comp")
    comp = lax.axis_index("comp")
    slots = tracer_mass.shape[0]

    groups = lax.broadcasted_iota(jnp.int32, (n_comp,), 0)
    count = jnp.sum(jnp.where(groups == comp, group_counts, 0))
    start = jnp.sum(jnp.where(groups < comp, group_counts, 0))
    numbers = lax.broadcasted_iota(jnp.int32, (slots, limiter_flags.shape[0]), 1)
    wanted = start + lax.broadcasted_iota(jnp.int32, (slots, limiter_flags.shape[0]), 0)
    flags = jnp.sum(jnp.where(numbers == wanted, limiter_flags[None, :], 0), 1)
    table = jnp.concatenate([count[None], flags])

    deal = dealing()
    f32 = jnp.float32
    vmem = pl.BlockSpec(memory_space=pltpu.VMEM)
    hbm = pl.BlockSpec(memory_space=pl.ANY)
    field = jax.ShapeDtypeStruct((ROWS, NX), f32)
    rows = pltpu.VMEM((STEPS, EXT, LEVELS, NX), f32)
    sides = pltpu.VMEM((slots, LEVELS, HALO, NX), f32)
    state = pltpu.VMEM((EXT, LEVELS, NX), f32)
    dma = pltpu.SemaphoreType.DMA
    out, *fields = pl.pallas_call(
        kernel,
        out_shape=(jax.ShapeDtypeStruct(tracer_mass.shape, f32), field, field, field),
        in_specs=[pl.BlockSpec(memory_space=pltpu.SMEM)] + [vmem] * 5 + [hbm],
        out_specs=(hbm, vmem, vmem, vmem),
        scratch_shapes=[
            pltpu.VMEM((n_comp, 3, EXT, NX), f32),
            pltpu.VMEM(tracer_mass.shape, f32),
            sides,
            sides,
            rows,
            rows,
            rows,
            state,
            state,
            state,
            pltpu.VMEM((TILES, LEVELS * 3 * EXT, 128), f32),
            pltpu.VMEM((3 * ROWS, NX), f32),
            state,
            pltpu.VMEM((TILES, LEVELS * ROWS, 128), f32),
            pltpu.VMEM((TILES, LEVELS * HALO, 128), f32),
            pltpu.VMEM((TILES, LEVELS * HALO, 128), f32),
            dma((slots,)),
            dma((slots,)),
            dma((2, slots)),
            dma((2, slots)),
            dma,
            dma,
            dma((2, n_comp)),
            dma((2, n_comp)),
            dma((2,)),
        ],
        compiler_params=pltpu.CompilerParams(
            collective_id=0, has_side_effects=True, vmem_limit_bytes=VMEM_LIMIT
        ),
    )(
        table,
        layer_mass.reshape(ROWS, NX),
        zonal_wind.reshape(ROWS, NX),
        merid_wind.reshape(ROWS, NX),
        deal,
        deal.T,
        tracer_mass,
    )
    return (out, *(field[None] for field in fields))


def solution(mesh):
    placed = (
        P("comp", None, "band", None),
        P("comp", "band", None),
        P("comp", "band", None),
        P("comp", "band", None),
        P(),
        P(),
    )
    return jax.shard_map(
        on_device,
        mesh=mesh,
        in_specs=placed,
        out_specs=placed[:4],
        check_vma=False,
    )
```

```python
import jax
import jax.numpy as jnp
import numpy as np
from jax import lax
from jax.experimental import pallas as pl
from jax.experimental.pallas import tpu as pltpu
from jax.sharding import PartitionSpec as P

STEPS = 4
HALO = 8
ROWS = 16
EXT = ROWS + 2 * HALO
LEVELS = 8
NX = 512
SLOTS = 24
BLOCK = 4
EARLY = 5
TILES = NX // 128
MESH_ID = pl.DeviceIdType.MESH
VMEM_LIMIT = 40 * 1024 * 1024

time_step = 0.1
gravity = 0.25
coriolis = 0.5
mass_floor = 0.5


def reach_of(step):
    return 2 * (STEPS - 1 - step)


def columns(i):
    return slice(128 * i, 128 * i + 128)


def level_rows(stage, first, stride):
    tiles = [
        stage[i, pl.ds(first, LEVELS, stride=stride), :] for i in range(NX // 128)
    ]
    return jnp.concatenate(tiles, axis=1)


def roll(value, shift):
    count = NX // 128
    tiles = [value[..., columns(i)] for i in range(count)]
    made = []
    for i in range(count):
        turns, at = divmod(i - shift, count)
        tile = tiles[at]
        if turns and tile.ndim == 3:
            turned = [pltpu.roll(tile[k], (-turns) % 128, 1) for k in range(tile.shape[0])]
            tile = jnp.stack(turned)
        elif turns:
            tile = pltpu.roll(tile, (-turns) % 128, 1)
        made.append(tile)
    return jnp.concatenate(made, axis=-1)


def dealing():
    place = np.arange(NX)
    source = (place % 128) * (NX // 128) + place // 128
    return (np.arange(NX)[:, None] == source[None, :]).astype(jnp.bfloat16)


def permuted(value, table):
    total = None
    rest = value
    for part in range(3):
        piece = rest.astype(jnp.bfloat16)
        moved = jnp.dot(piece, table, preferred_element_type=jnp.float32)
        total = moved if total is None else total + moved
        rest = rest - piece.astype(jnp.float32)
    return total


def dynamics(fields, back_ref, inv_ref, east_ref, south_ref, last_refs, h_buf, u_buf, v_buf, stage, picked_ref):
    level, band = lax.axis_index("comp"), lax.axis_index("band")
    first_row, total_rows = band * ROWS, lax.axis_size("band") * ROWS
    stride = 3 * EXT

    for k in range(LEVELS):
        for f in range(3):
            rows = slice((k * 3 + f) * EXT, (k * 3 + f + 1) * EXT)
            for i in range(TILES):
                stage[i, rows, :] = fields[k, f, :, columns(i)]

    @pl.loop(0, EXT)
    def _(j):
        for f, buf in enumerate((h_buf, u_buf, v_buf)):
            buf[j] = level_rows(stage, f * EXT + j, stride)

    depth = lax.broadcasted_iota(jnp.int32, (LEVELS, NX), 0)

    def geopot(h):
        total = h
        for gap in (1, 2, 4):
            moved = pltpu.roll(total, LEVELS - gap, 0)
            total = total + jnp.where(depth < LEVELS - gap, moved, 0.0)
        return gravity * total

    def south_flux(h_a, h_b, v_a, v_b, face):
        at = first_row + face - HALO
        inside = jnp.logical_and(at > 0, at < total_rows)
        scale = jnp.where(inside, 0.25 * time_step, 0.0)
        return scale * ((v_a + v_b) * (h_a + h_b))

    for step in range(STEPS):
        reach = reach_of(step)
        low, high = HALO - reach, HALO + ROWS + reach
        for j in (low - 2, low - 1, high, high + 1):
            inv_ref[step, j] = 1.0 / jnp.maximum(h_buf[j], mass_floor)
        h_before, h_here = h_buf[low - 1], h_buf[low]
        v_before, v_here = v_buf[low - 1], v_buf[low]
        south = south_flux(h_before, h_here, v_before, v_here, low)
        south_ref[step, low] = south

        def row(j, carry, step=step):
            h, v, geo_before, geo, south = carry
            h_after, v_after, u = h_buf[j + 1], v_buf[j + 1], u_buf[j]
            geo_after = geopot(h_after)
            south_after = south_flux(h, h_after, v, v_after, j + 1)
            east = (0.25 * time_step) * ((u + roll(u, -1)) * (h + roll(h, -1)))
            inv_ref[step, j] = 1.0 / jnp.maximum(h, mass_floor)
            east_ref[step, j] = east
            south_ref[step, j + 1] = south_after
            h_buf[j] = h - ((east - roll(east, 1)) + (south_after - south))
            u_buf[j] = u + time_step * (coriolis * v - 0.5 * (roll(geo, -1) - roll(geo, 1)))
            v_buf[j] = v - time_step * (coriolis * u + 0.5 * (geo_after - geo_before))
            return h_after, v_after, geo, geo_after, south_after

        carry = (h_here, v_here, geopot(h_before), geopot(h_here), south)
        for j in range(low, high):
            carry = row(j, carry)

    own = lax.broadcasted_iota(jnp.int32, (LEVELS, NX), 0) == level
    for f, buf in enumerate((h_buf, u_buf, v_buf)):
        for j in range(ROWS):
            picked = jnp.where(own, buf[HALO + j], 0.0)
            picked_ref[pl.ds(f * ROWS + j, 1), :] = jnp.sum(picked, axis=0, keepdims=True)
    last = permuted(picked_ref[...], back_ref[...])
    for f in range(3):
        last_refs[f][...] = last[f * ROWS : (f + 1) * ROWS]


def advance_slot(limited, buf, stage, inv_ref, east_ref, south_ref):
    def face(a_out, a, b, b_out):
        raw = (7.0 / 12.0) * (a + b) - (1.0 / 12.0) * (a_out + b_out)
        bounded = jnp.maximum(jnp.minimum(raw, jnp.maximum(a, b)), jnp.minimum(a, b))
        return jnp.where(limited, bounded, raw)

    for step in range(STEPS):
        reach = reach_of(step)
        low, high = HALO - reach, HALO + ROWS + reach

        def ratios(j, n, step=step):
            return buf[j : j + n] * inv_ref[step, j : j + n]

        r = ratios(low - 2, 4)
        south = south_ref[step, low : low + 1] * face(r[0:1], r[1:2], r[2:3], r[3:4])
        r = r[1:]
        for j in range(low, high, BLOCK):
            r = jnp.concatenate([r, ratios(j + 2, BLOCK)], axis=0)
            here = r[1 : BLOCK + 1]
            after = south_ref[step, j + 1 : j + 1 + BLOCK] * face(
                r[0:BLOCK], here, r[2 : BLOCK + 2], r[3 : BLOCK + 3]
            )
            south = jnp.concatenate([south, after], axis=0)
            east = east_ref[step, j : j + BLOCK] * face(
                roll(here, 1), here, roll(here, -1), roll(here, -2)
            )
            new = buf[j : j + BLOCK] - ((east - roll(east, 1)) + (after - south[:BLOCK]))
            if step < STEPS - 1:
                buf[j : j + BLOCK] = new
            else:
                for k in range(BLOCK):
                    for i in range(TILES):
                        place = pl.ds(j + k - HALO, LEVELS, stride=ROWS)
                        stage[i, place, :] = new[k][:, columns(i)]
            r, south = r[BLOCK:], south[BLOCK:]


def kernel(
    counts_ref, flags_ref, h_ref, u_ref, v_ref, deal_ref, back_ref, mass_ref,
    out_ref, h_out, u_out, v_out,
    fields, masses, lows, highs, inv_ref, east_ref, south_ref,
    h_buf, u_buf, v_buf, g_stage, picked_ref, buf, dealt, stage, low_stage, high_stage,
    load_sem, rows_send, rows_recv, side_send, side_recv,
    field_send, field_recv, swap_sem,
):
    n_comp, n_band = lax.axis_size("comp"), lax.axis_size("band")
    level, band = lax.axis_index("comp"), lax.axis_index("band")
    core = lax.rem(band, 2)
    beside = level + 1 - 2 * lax.rem(level, 2)
    sibling = band + 1 - 2 * core
    has_low, has_high = band > 0, band < n_band - 1
    outer = lax.rem(band + n_band - 1 + 2 * core, n_band)
    has_outer = jnp.logical_and(band > 0, band < n_band - 1)
    slots = masses.shape[0]

    count, start = counts_ref[level], 0
    for g in range(n_comp):
        start = start + jnp.where(g < level, counts_ref[g], 0)
    last_flag = flags_ref.shape[0] - 1

    def load(t):
        return pltpu.make_async_copy(mass_ref.at[t], masses.at[t], load_sem.at[t])

    def down(t):
        return pltpu.make_async_remote_copy(
            src_ref=mass_ref.at[t, :, pl.ds(0, HALO), :],
            dst_ref=highs.at[t],
            send_sem=rows_send.at[0, t],
            recv_sem=rows_recv.at[0, t],
            device_id={"band": lax.max(band - 1, 0)},
            device_id_type=MESH_ID,
        )

    def up(t):
        return pltpu.make_async_remote_copy(
            src_ref=mass_ref.at[t, :, pl.ds(HALO, HALO), :],
            dst_ref=lows.at[t],
            send_sem=rows_send.at[1, t],
            recv_sem=rows_recv.at[1, t],
            device_id={"band": lax.min(band + 1, n_band - 1)},
            device_id_type=MESH_ID,
        )

    def send_rows(first, last):
        @pl.when(has_low)
        def _():
            @pl.loop(first, last)
            def _(t):
                down(t).start()

        @pl.when(has_high)
        def _():
            @pl.loop(first, last)
            def _(t):
                up(t).start()

    barrier = pltpu.get_barrier_semaphore()
    peers = [{"comp": beside}, {"band": sibling}]
    peers += [{"comp": lax.rem(level + 2 * p, n_comp)} for p in range(1, n_comp // 2)]
    for peer in peers:
        pl.semaphore_signal(barrier, inc=1, device_id=peer, device_id_type=MESH_ID)

    @pl.when(has_outer)
    def _():
        pl.semaphore_signal(barrier, inc=1, device_id={"band": outer}, device_id_type=MESH_ID)

    @pl.loop(0, slots)
    def _(t):
        load(t).start()

    own = jnp.concatenate([h_ref[...], u_ref[...], v_ref[...]], axis=0)
    own = permuted(own, deal_ref[...])
    for f in range(3):
        fields[level, f, HALO : HALO + ROWS, :] = own[f * ROWS : (f + 1) * ROWS]

    edge = pl.multiple_of(2 * (HALO + HALO // 2) * core, HALO)

    @pl.when(jnp.logical_not(has_outer))
    def _():
        fields[level, :, pl.ds(edge, HALO), :] = jnp.zeros((3, HALO, NX), jnp.float32)

    @pl.when(jnp.logical_not(has_low))
    def _():
        lows[...] = jnp.zeros_like(lows)

    @pl.when(jnp.logical_not(has_high))
    def _():
        highs[...] = jnp.zeros_like(highs)

    pl.semaphore_wait(barrier, len(peers) + has_outer.astype(jnp.int32))

    side = pltpu.make_async_remote_copy(
        src_ref=fields.at[level, :, pl.ds(pl.multiple_of(HALO + HALO * core, HALO), HALO), :],
        dst_ref=fields.at[level, :, pl.ds(pl.multiple_of(3 * HALO * (1 - core), HALO), HALO), :],
        send_sem=side_send,
        recv_sem=side_recv,
        device_id={"band": outer},
        device_id_type=MESH_ID,
    )

    @pl.when(has_outer)
    def _():
        side.start()

    def piece(k, owner, target, lane):
        rows = pl.ds(HALO, ROWS) if k == 0 else pl.ds(edge, HALO)
        return pltpu.make_async_remote_copy(
            src_ref=fields.at[owner, :, rows, :],
            dst_ref=fields.at[owner, :, rows, :],
            send_sem=field_send.at[k, lane],
            recv_sem=field_recv.at[k, lane],
            device_id={"comp": target},
            device_id_type=MESH_ID,
        )

    ring = range(1, n_comp // 2)

    def to_all(k):
        sends = [piece(k, level, beside, 0)]
        sends += [piece(k, level, lax.rem(level + 2 * p, n_comp), p) for p in ring]
        return sends

    def passed_on(k):
        return [piece(k, beside, lax.rem(level + 2 * p, n_comp), n_comp // 2 + p) for p in ring]

    def arriving(k):
        far = [lax.rem(level + n_comp - 2 * p, n_comp) for p in ring]
        waits = [piece(k, owner, beside, p) for p, owner in zip(ring, far)]
        far = [lax.rem(beside + n_comp - 2 * p, n_comp) for p in ring]
        return waits + [piece(k, owner, beside, n_comp // 2 + p) for p, owner in zip(ring, far)]

    def deal_slots(first, last):
        @pl.loop(first, last)
        def _(t):
            load(t).wait()
            block = permuted(masses[t].reshape(LEVELS * ROWS, NX), deal_ref[...])
            for i in range(TILES):
                dealt[t, i] = block[:, columns(i)]

    for send in to_all(0):
        send.start()
    deal_slots(0, 4)

    @pl.when(has_outer)
    def _():
        side.wait_recv()

    for send in to_all(1):
        send.start()
    for k in range(2):
        piece(k, beside, beside, 0).wait_recv()
        for send in passed_on(k):
            send.start()
    send_rows(0, EARLY)
    deal_slots(4, slots)
    for wait in arriving(0):
        wait.wait_recv()

    swap = pltpu.make_async_remote_copy(
        src_ref=fields.at[:, :, pl.ds(pl.multiple_of(2 * HALO - HALO * core, HALO), HALO), :],
        dst_ref=fields.at[:, :, pl.ds(pl.multiple_of(3 * HALO * core, HALO), HALO), :],
        send_sem=swap_sem.at[0],
        recv_sem=swap_sem.at[1],
        device_id={"band": sibling},
        device_id_type=MESH_ID,
    )
    swap.start()
    send_rows(EARLY, slots)
    for wait in arriving(1):
        wait.wait_recv()
    swap.wait_recv()

    dynamics(
        fields, back_ref, inv_ref, east_ref, south_ref, (h_out, u_out, v_out),
        h_buf, u_buf, v_buf, g_stage, picked_ref,
    )

    @pl.loop(0, slots)
    def _(t):
        @pl.when(has_low)
        def _():
            up(t).wait_recv()

        @pl.when(has_high)
        def _():
            down(t).wait_recv()

        sides = (LEVELS * HALO, NX)
        blocks = (
            (lows[t].reshape(sides), low_stage),
            (highs[t].reshape(sides), high_stage),
        )
        for block, to in blocks:
            moved = permuted(block, deal_ref[...])
            for i in range(TILES):
                to[i] = moved[:, columns(i)]
        for j in range(HALO):
            buf[j] = level_rows(low_stage, j, HALO)
            buf[HALO + ROWS + j] = level_rows(high_stage, j, HALO)
        for j in range(ROWS):
            buf[HALO + j] = level_rows(dealt.at[t], j, ROWS)
        limited = flags_ref[jnp.minimum(start + t, last_flag)] > 0
        advance_slot(limited, buf, stage, inv_ref, east_ref, south_ref)
        final = jnp.concatenate([stage[i] for i in range(TILES)], axis=1)
        final = permuted(final, back_ref[...])
        final = jnp.where(t < count, final, 0.0)
        out_ref[t] = final.reshape(LEVELS, ROWS, NX)

    @pl.loop(0, slots)
    def _(t):
        @pl.when(has_low)
        def _():
            down(t).wait_send()

        @pl.when(has_high)
        def _():
            up(t).wait_send()

    @pl.when(has_outer)
    def _():
        side.wait_send()

    swap.wait_send()
    for k in range(2):
        for send in to_all(k) + passed_on(k):
            send.wait_send()


def on_device(tracer_mass, layer_mass, zonal_wind, merid_wind, group_counts, limiter_flags):
    n_comp = lax.axis_size("comp")
    slots = tracer_mass.shape[0]

    deal = dealing()
    f32 = jnp.float32
    vmem = pl.BlockSpec(memory_space=pltpu.VMEM)
    hbm = pl.BlockSpec(memory_space=pl.ANY)
    field = jax.ShapeDtypeStruct((ROWS, NX), f32)
    rows = pltpu.VMEM((STEPS, EXT, LEVELS, NX), f32)
    sides = pltpu.VMEM((slots, LEVELS, HALO, NX), f32)
    state = pltpu.VMEM((EXT, LEVELS, NX), f32)
    dma = pltpu.SemaphoreType.DMA
    out, *fields = pl.pallas_call(
        kernel,
        out_shape=(jax.ShapeDtypeStruct(tracer_mass.shape, f32), field, field, field),
        in_specs=[pl.BlockSpec(memory_space=pltpu.SMEM)] * 2 + [vmem] * 5 + [hbm],
        out_specs=(vmem, vmem, vmem, vmem),
        scratch_shapes=[
            pltpu.VMEM((n_comp, 3, EXT, NX), f32),
            pltpu.VMEM(tracer_mass.shape, f32),
            sides,
            sides,
            rows,
            rows,
            rows,
            state,
            state,
            state,
            pltpu.VMEM((TILES, LEVELS * 3 * EXT, 128), f32),
            pltpu.VMEM((3 * ROWS, NX), f32),
            state,
            pltpu.VMEM((slots, TILES, LEVELS * ROWS, 128), f32),
            pltpu.VMEM((TILES, LEVELS * ROWS, 128), f32),
            pltpu.VMEM((TILES, LEVELS * HALO, 128), f32),
            pltpu.VMEM((TILES, LEVELS * HALO, 128), f32),
            dma((slots,)),
            dma((2, slots)),
            dma((2, slots)),
            dma,
            dma,
            dma((2, n_comp)),
            dma((2, n_comp)),
            dma((2,)),
        ],
        compiler_params=pltpu.CompilerParams(
            collective_id=0, has_side_effects=True, vmem_limit_bytes=VMEM_LIMIT
        ),
    )(
        group_counts,
        limiter_flags,
        layer_mass.reshape(ROWS, NX),
        zonal_wind.reshape(ROWS, NX),
        merid_wind.reshape(ROWS, NX),
        jnp.asarray(deal),
        jnp.asarray(deal.T),
        tracer_mass,
    )
    return (out, *(field[None] for field in fields))


def solution(mesh):
    placed = (
        P("comp", None, "band", None),
        P("comp", "band", None),
        P("comp", "band", None),
        P("comp", "band", None),
        P(),
        P(),
    )
    return jax.shard_map(
        on_device,
        mesh=mesh,
        in_specs=placed,
        out_specs=placed[:4],
        check_vma=False,
    )
```

```python
import jax
import jax.numpy as jnp
from jax import lax
from jax.experimental import pallas as pl
from jax.experimental.pallas import tpu as pltpu
from jax.sharding import PartitionSpec as P

STEPS = 4
HALO = 8
ROWS = 16
EXT = ROWS + 2 * HALO
LEVELS = 8
NX = 512
SLOTS = 24
BLOCK = 4
EARLY = 5
TILES = NX // 128
MESH_ID = pl.DeviceIdType.MESH
VMEM_LIMIT = 45 * 1024 * 1024

time_step = 0.1
gravity = 0.25
coriolis = 0.5
mass_floor = 0.5


def reach_of(step):
    return 2 * (STEPS - 1 - step)


def columns(i):
    return slice(128 * i, 128 * i + 128)


def level_rows(stage, first, stride):
    tiles = [
        stage[i, pl.ds(first, LEVELS, stride=stride), :] for i in range(NX // 128)
    ]
    return jnp.concatenate(tiles, axis=1)


def roll(value, shift):
    count = NX // 128
    tiles = [value[..., columns(i)] for i in range(count)]
    made = []
    for i in range(count):
        turns, at = divmod(i - shift, count)
        tile = tiles[at]
        if turns and tile.ndim == 3:
            turned = [pltpu.roll(tile[k], (-turns) % 128, 1) for k in range(tile.shape[0])]
            tile = jnp.stack(turned)
        elif turns:
            tile = pltpu.roll(tile, (-turns) % 128, 1)
        made.append(tile)
    return jnp.concatenate(made, axis=-1)


def make_dealing(table_ref, backward):
    chunk = 32

    @pl.loop(0, NX // chunk)
    def _(c):
        source = lax.broadcasted_iota(jnp.int32, (chunk, NX), 0) + c * chunk
        place = lax.broadcasted_iota(jnp.int32, (chunk, NX), 1)
        if backward:
            source, place = place, source
        dealt = (place & 127) * TILES + (place >> 7) == source
        rows = pl.ds(pl.multiple_of(c * chunk, chunk), chunk)
        table_ref[rows, :] = jnp.where(dealt, 1.0, 0.0).astype(jnp.bfloat16)


def permuted(value, table):
    total = None
    rest = value
    for part in range(3):
        piece = rest.astype(jnp.bfloat16)
        moved = jnp.dot(piece, table, preferred_element_type=jnp.float32)
        total = moved if total is None else total + moved
        rest = rest - piece.astype(jnp.float32)
    return total


def dynamics(fields, back_ref, inv_ref, east_ref, south_ref, last_ref, h_buf, u_buf, v_buf, stage, picked_ref):
    level, band = lax.axis_index("comp"), lax.axis_index("band")
    first_row, total_rows = band * ROWS, lax.axis_size("band") * ROWS
    stride = 3 * EXT

    for k in range(LEVELS):
        for f in range(3):
            rows = slice((k * 3 + f) * EXT, (k * 3 + f + 1) * EXT)
            for i in range(TILES):
                stage[i, rows, :] = fields[k, f, :, columns(i)]

    @pl.loop(0, EXT)
    def _(j):
        for f, buf in enumerate((h_buf, u_buf, v_buf)):
            buf[j] = level_rows(stage, f * EXT + j, stride)

    depth = lax.broadcasted_iota(jnp.int32, (LEVELS, NX), 0)

    def geopot(h):
        total = h
        for gap in (1, 2, 4):
            moved = pltpu.roll(total, LEVELS - gap, 0)
            total = total + jnp.where(depth < LEVELS - gap, moved, 0.0)
        return gravity * total

    def south_flux(h_a, h_b, v_a, v_b, face):
        at = first_row + face - HALO
        inside = jnp.logical_and(at > 0, at < total_rows)
        scale = jnp.where(inside, 0.25 * time_step, 0.0)
        return scale * ((v_a + v_b) * (h_a + h_b))

    for step in range(STEPS):
        reach = reach_of(step)
        low, high = HALO - reach, HALO + ROWS + reach
        for j in (low - 2, low - 1, high, high + 1):
            inv_ref[step, j] = 1.0 / jnp.maximum(h_buf[j], mass_floor)
        h_before, h_here = h_buf[low - 1], h_buf[low]
        v_before, v_here = v_buf[low - 1], v_buf[low]
        south = south_flux(h_before, h_here, v_before, v_here, low)
        south_ref[step, low] = south

        def row(j, carry, step=step):
            h, v, geo_before, geo, south = carry
            h_after, v_after, u = h_buf[j + 1], v_buf[j + 1], u_buf[j]
            geo_after = geopot(h_after)
            south_after = south_flux(h, h_after, v, v_after, j + 1)
            east = (0.25 * time_step) * ((u + roll(u, -1)) * (h + roll(h, -1)))
            inv_ref[step, j] = 1.0 / jnp.maximum(h, mass_floor)
            east_ref[step, j] = east
            south_ref[step, j + 1] = south_after
            h_buf[j] = h - ((east - roll(east, 1)) + (south_after - south))
            u_buf[j] = u + time_step * (coriolis * v - 0.5 * (roll(geo, -1) - roll(geo, 1)))
            v_buf[j] = v - time_step * (coriolis * u + 0.5 * (geo_after - geo_before))
            return h_after, v_after, geo, geo_after, south_after

        carry = (h_here, v_here, geopot(h_before), geopot(h_here), south)
        for j in range(low, high):
            carry = row(j, carry)

    own = lax.broadcasted_iota(jnp.int32, (LEVELS, NX), 0) == level
    for f, buf in enumerate((h_buf, u_buf, v_buf)):
        for j in range(ROWS):
            picked = jnp.where(own, buf[HALO + j], 0.0)
            picked_ref[pl.ds(f * ROWS + j, 1), :] = jnp.sum(picked, axis=0, keepdims=True)
    last_ref[...] = permuted(picked_ref[...], back_ref[...])


def advance_slot(limited, buf, stage, inv_ref, east_ref, south_ref):
    def face(a_out, a, b, b_out):
        raw = (7.0 / 12.0) * (a + b) - (1.0 / 12.0) * (a_out + b_out)
        bounded = jnp.maximum(jnp.minimum(raw, jnp.maximum(a, b)), jnp.minimum(a, b))
        return jnp.where(limited, bounded, raw)

    for step in range(STEPS):
        reach = reach_of(step)
        low, high = HALO - reach, HALO + ROWS + reach

        def ratios(j, n, step=step):
            return buf[j : j + n] * inv_ref[step, j : j + n]

        r = ratios(low - 2, 4)
        south = south_ref[step, low : low + 1] * face(r[0:1], r[1:2], r[2:3], r[3:4])
        r = r[1:]
        for j in range(low, high, BLOCK):
            r = jnp.concatenate([r, ratios(j + 2, BLOCK)], axis=0)
            here = r[1 : BLOCK + 1]
            after = south_ref[step, j + 1 : j + 1 + BLOCK] * face(
                r[0:BLOCK], here, r[2 : BLOCK + 2], r[3 : BLOCK + 3]
            )
            south = jnp.concatenate([south, after], axis=0)
            east = east_ref[step, j : j + BLOCK] * face(
                roll(here, 1), here, roll(here, -1), roll(here, -2)
            )
            new = buf[j : j + BLOCK] - ((east - roll(east, 1)) + (after - south[:BLOCK]))
            if step < STEPS - 1:
                buf[j : j + BLOCK] = new
            else:
                for k in range(BLOCK):
                    for i in range(TILES):
                        place = pl.ds(j + k - HALO, LEVELS, stride=ROWS)
                        stage[i, place, :] = new[k][:, columns(i)]
            r, south = r[BLOCK:], south[BLOCK:]


def kernel(
    counts_ref, flags_ref, h_ref, u_ref, v_ref, mass_ref,
    out_ref, last_ref,
    own_ref, deal_ref, back_ref, fields, masses, lows, highs, inv_ref, east_ref, south_ref,
    h_buf, u_buf, v_buf, g_stage, picked_ref, buf, dealt, stage, low_stage, high_stage,
    load_sem, rows_send, rows_recv, side_send, side_recv,
    field_send, field_recv, swap_sem, first_sem,
):
    n_comp, n_band = lax.axis_size("comp"), lax.axis_size("band")
    level, band = lax.axis_index("comp"), lax.axis_index("band")
    core = lax.rem(band, 2)
    beside = level + 1 - 2 * lax.rem(level, 2)
    sibling = band + 1 - 2 * core
    has_low, has_high = band > 0, band < n_band - 1
    outer = lax.rem(band + n_band - 1 + 2 * core, n_band)
    has_outer = jnp.logical_and(band > 0, band < n_band - 1)
    slots = masses.shape[0]

    count, start = counts_ref[level], 0
    for g in range(n_comp):
        start = start + jnp.where(g < level, counts_ref[g], 0)
    last_flag = flags_ref.shape[0] - 1

    def load(t):
        return pltpu.make_async_copy(mass_ref.at[t], masses.at[t], load_sem.at[t])

    def down(t):
        return pltpu.make_async_remote_copy(
            src_ref=mass_ref.at[t, :, pl.ds(0, HALO), :],
            dst_ref=highs.at[t],
            send_sem=rows_send.at[0, t],
            recv_sem=rows_recv.at[0, t],
            device_id={"band": lax.max(band - 1, 0)},
            device_id_type=MESH_ID,
        )

    def up(t):
        return pltpu.make_async_remote_copy(
            src_ref=mass_ref.at[t, :, pl.ds(HALO, HALO), :],
            dst_ref=lows.at[t],
            send_sem=rows_send.at[1, t],
            recv_sem=rows_recv.at[1, t],
            device_id={"band": lax.min(band + 1, n_band - 1)},
            device_id_type=MESH_ID,
        )

    def send_rows(first, last):
        @pl.when(has_low)
        def _():
            @pl.loop(first, last)
            def _(t):
                down(t).start()

        @pl.when(has_high)
        def _():
            @pl.loop(first, last)
            def _(t):
                up(t).start()

    firsts = []
    for f, ref in enumerate((h_ref, u_ref, v_ref)):
        firsts.append((ref, own_ref.at[pl.ds(f * ROWS, ROWS), :]))
    firsts = [
        pltpu.make_async_copy(src, dst, first_sem.at[n]) for n, (src, dst) in enumerate(firsts)
    ]
    for first in firsts:
        first.start()

    barrier = pltpu.get_barrier_semaphore()
    peers = [{"comp": beside}, {"band": sibling}]
    peers += [{"comp": lax.rem(level + 2 * p, n_comp)} for p in range(1, n_comp // 2)]
    for peer in peers:
        pl.semaphore_signal(barrier, inc=1, device_id=peer, device_id_type=MESH_ID)

    @pl.when(has_outer)
    def _():
        pl.semaphore_signal(barrier, inc=1, device_id={"band": outer}, device_id_type=MESH_ID)

    @pl.loop(0, slots)
    def _(t):
        load(t).start()

    make_dealing(deal_ref, False)
    for first in firsts:
        first.wait()
    own = permuted(own_ref[...], deal_ref[...])
    for f in range(3):
        fields[level, f, HALO : HALO + ROWS, :] = own[f * ROWS : (f + 1) * ROWS]

    edge = pl.multiple_of(2 * (HALO + HALO // 2) * core, HALO)

    @pl.when(jnp.logical_not(has_outer))
    def _():
        fields[level, :, pl.ds(edge, HALO), :] = jnp.zeros((3, HALO, NX), jnp.float32)

    @pl.when(jnp.logical_not(has_low))
    def _():
        lows[...] = jnp.zeros_like(lows)

    @pl.when(jnp.logical_not(has_high))
    def _():
        highs[...] = jnp.zeros_like(highs)

    pl.semaphore_wait(barrier, len(peers) + has_outer.astype(jnp.int32))

    side = pltpu.make_async_remote_copy(
        src_ref=fields.at[level, :, pl.ds(pl.multiple_of(HALO + HALO * core, HALO), HALO), :],
        dst_ref=fields.at[level, :, pl.ds(pl.multiple_of(3 * HALO * (1 - core), HALO), HALO), :],
        send_sem=side_send,
        recv_sem=side_recv,
        device_id={"band": outer},
        device_id_type=MESH_ID,
    )

    @pl.when(has_outer)
    def _():
        side.start()

    def piece(k, owner, target, lane):
        rows = pl.ds(HALO, ROWS) if k == 0 else pl.ds(edge, HALO)
        return pltpu.make_async_remote_copy(
            src_ref=fields.at[owner, :, rows, :],
            dst_ref=fields.at[owner, :, rows, :],
            send_sem=field_send.at[k, lane],
            recv_sem=field_recv.at[k, lane],
            device_id={"comp": target},
            device_id_type=MESH_ID,
        )

    ring = range(1, n_comp // 2)

    def to_all(k):
        sends = [piece(k, level, beside, 0)]
        sends += [piece(k, level, lax.rem(level + 2 * p, n_comp), p) for p in ring]
        return sends

    def passed_on(k):
        return [piece(k, beside, lax.rem(level + 2 * p, n_comp), n_comp // 2 + p) for p in ring]

    def arriving(k):
        far = [lax.rem(level + n_comp - 2 * p, n_comp) for p in ring]
        waits = [piece(k, owner, beside, p) for p, owner in zip(ring, far)]
        far = [lax.rem(beside + n_comp - 2 * p, n_comp) for p in ring]
        return waits + [piece(k, owner, beside, n_comp // 2 + p) for p, owner in zip(ring, far)]

    def deal_slots(first, last):
        @pl.loop(first, last)
        def _(t):
            load(t).wait()
            block = permuted(masses[t].reshape(LEVELS * ROWS, NX), deal_ref[...])
            for i in range(TILES):
                dealt[t, i] = block[:, columns(i)]

    for send in to_all(0):
        send.start()
    make_dealing(back_ref, True)

    @pl.when(has_outer)
    def _():
        side.wait_recv()

    for send in to_all(1):
        send.start()
    for k in range(2):
        piece(k, beside, beside, 0).wait_recv()
        for send in passed_on(k):
            send.start()
    send_rows(0, EARLY)
    deal_slots(0, slots)
    for wait in arriving(0):
        wait.wait_recv()

    swap = pltpu.make_async_remote_copy(
        src_ref=fields.at[:, :, pl.ds(pl.multiple_of(2 * HALO - HALO * core, HALO), HALO), :],
        dst_ref=fields.at[:, :, pl.ds(pl.multiple_of(3 * HALO * core, HALO), HALO), :],
        send_sem=swap_sem.at[0],
        recv_sem=swap_sem.at[1],
        device_id={"band": sibling},
        device_id_type=MESH_ID,
    )
    swap.start()
    send_rows(EARLY, slots)
    for wait in arriving(1):
        wait.wait_recv()
    swap.wait_recv()

    dynamics(
        fields, back_ref, inv_ref, east_ref, south_ref, last_ref,
        h_buf, u_buf, v_buf, g_stage, picked_ref,
    )

    @pl.loop(0, slots)
    def _(t):
        @pl.when(has_low)
        def _():
            up(t).wait_recv()

        @pl.when(has_high)
        def _():
            down(t).wait_recv()

        sides = (LEVELS * HALO, NX)
        blocks = (
            (lows[t].reshape(sides), low_stage),
            (highs[t].reshape(sides), high_stage),
        )
        for block, to in blocks:
            moved = permuted(block, deal_ref[...])
            for i in range(TILES):
                to[i] = moved[:, columns(i)]
        for j in range(HALO):
            buf[j] = level_rows(low_stage, j, HALO)
            buf[HALO + ROWS + j] = level_rows(high_stage, j, HALO)
        for j in range(ROWS):
            buf[HALO + j] = level_rows(dealt.at[t], j, ROWS)
        limited = flags_ref[jnp.minimum(start + t, last_flag)] > 0
        advance_slot(limited, buf, stage, inv_ref, east_ref, south_ref)
        final = jnp.concatenate([stage[i] for i in range(TILES)], axis=1)
        final = permuted(final, back_ref[...])
        final = jnp.where(t < count, final, 0.0)
        out_ref[t] = final.reshape(LEVELS, ROWS, NX)

    @pl.loop(0, slots)
    def _(t):
        @pl.when(has_low)
        def _():
            down(t).wait_send()

        @pl.when(has_high)
        def _():
            up(t).wait_send()

    @pl.when(has_outer)
    def _():
        side.wait_send()

    swap.wait_send()
    for k in range(2):
        for send in to_all(k) + passed_on(k):
            send.wait_send()


def on_device(tracer_mass, layer_mass, zonal_wind, merid_wind, group_counts, limiter_flags):
    n_comp = lax.axis_size("comp")
    slots = tracer_mass.shape[0]

    f32 = jnp.float32
    vmem = pl.BlockSpec(memory_space=pltpu.VMEM)
    hbm = pl.BlockSpec(memory_space=pl.ANY)
    rows = pltpu.VMEM((STEPS, EXT, LEVELS, NX), f32)
    sides = pltpu.VMEM((slots, LEVELS, HALO, NX), f32)
    state = pltpu.VMEM((EXT, LEVELS, NX), f32)
    dma = pltpu.SemaphoreType.DMA
    out, last = pl.pallas_call(
        kernel,
        out_shape=(
            jax.ShapeDtypeStruct(tracer_mass.shape, f32),
            jax.ShapeDtypeStruct((3 * ROWS, NX), f32),
        ),
        in_specs=[pl.BlockSpec(memory_space=pltpu.SMEM)] * 2 + [hbm] * 4,
        out_specs=(vmem, vmem),
        scratch_shapes=[
            pltpu.VMEM((3 * ROWS, NX), f32),
            pltpu.VMEM((NX, NX), jnp.bfloat16),
            pltpu.VMEM((NX, NX), jnp.bfloat16),
            pltpu.VMEM((n_comp, 3, EXT, NX), f32),
            pltpu.VMEM(tracer_mass.shape, f32),
            sides,
            sides,
            rows,
            rows,
            rows,
            state,
            state,
            state,
            pltpu.VMEM((TILES, LEVELS * 3 * EXT, 128), f32),
            pltpu.VMEM((3 * ROWS, NX), f32),
            state,
            pltpu.VMEM((slots, TILES, LEVELS * ROWS, 128), f32),
            pltpu.VMEM((TILES, LEVELS * ROWS, 128), f32),
            pltpu.VMEM((TILES, LEVELS * HALO, 128), f32),
            pltpu.VMEM((TILES, LEVELS * HALO, 128), f32),
            dma((slots,)),
            dma((2, slots)),
            dma((2, slots)),
            dma,
            dma,
            dma((2, n_comp)),
            dma((2, n_comp)),
            dma((2,)),
            dma((3,)),
        ],
        compiler_params=pltpu.CompilerParams(
            collective_id=0, has_side_effects=True, vmem_limit_bytes=VMEM_LIMIT
        ),
    )(
        group_counts,
        limiter_flags,
        layer_mass.reshape(ROWS, NX),
        zonal_wind.reshape(ROWS, NX),
        merid_wind.reshape(ROWS, NX),
        tracer_mass,
    )
    last = last.reshape(3, 1, ROWS, NX)
    return out, last[0], last[1], last[2]


def solution(mesh):
    placed = (
        P("comp", None, "band", None),
        P("comp", "band", None),
        P("comp", "band", None),
        P("comp", "band", None),
        P(),
        P(),
    )
    return jax.shard_map(
        on_device,
        mesh=mesh,
        in_specs=placed,
        out_specs=placed[:4],
        check_vma=False,
    )
```

```python
import jax
import jax.numpy as jnp
from jax import lax
from jax.experimental import pallas as pl
from jax.experimental.pallas import tpu as pltpu
from jax.sharding import PartitionSpec as P

STEPS = 4
HALO = 8
ROWS = 16
EXT = ROWS + 2 * HALO
LEVELS = 8
NX = 512
SLOTS = 24
BLOCK = 4
EARLY = 5
AHEAD = 3
TILES = NX // 128
MESH_ID = pl.DeviceIdType.MESH
VMEM_LIMIT = 45 * 1024 * 1024

time_step = 0.1
gravity = 0.25
coriolis = 0.5
mass_floor = 0.5


def reach_of(step):
    return 2 * (STEPS - 1 - step)


def columns(i):
    return slice(128 * i, 128 * i + 128)


def level_rows(stage, first, stride):
    tiles = [
        stage[i, pl.ds(first, LEVELS, stride=stride), :] for i in range(NX // 128)
    ]
    return jnp.concatenate(tiles, axis=1)


def roll(value, shift):
    count = NX // 128
    tiles = [value[..., columns(i)] for i in range(count)]
    made = []
    for i in range(count):
        turns, at = divmod(i - shift, count)
        tile = tiles[at]
        if turns and tile.ndim == 3:
            turned = [pltpu.roll(tile[k], (-turns) % 128, 1) for k in range(tile.shape[0])]
            tile = jnp.stack(turned)
        elif turns:
            tile = pltpu.roll(tile, (-turns) % 128, 1)
        made.append(tile)
    return jnp.concatenate(made, axis=-1)


def make_dealing(table_ref, backward):
    chunk = 32

    @pl.loop(0, NX // chunk)
    def _(c):
        source = lax.broadcasted_iota(jnp.int32, (chunk, NX), 0) + c * chunk
        place = lax.broadcasted_iota(jnp.int32, (chunk, NX), 1)
        if backward:
            source, place = place, source
        dealt = (place & 127) * TILES + (place >> 7) == source
        rows = pl.ds(pl.multiple_of(c * chunk, chunk), chunk)
        table_ref[rows, :] = jnp.where(dealt, 1.0, 0.0).astype(jnp.bfloat16)


def permuted(value, table):
    total = None
    rest = value
    for part in range(3):
        piece = rest.astype(jnp.bfloat16)
        moved = jnp.dot(piece, table, preferred_element_type=jnp.float32)
        total = moved if total is None else total + moved
        rest = rest - piece.astype(jnp.float32)
    return total


def dynamics(fields, back_ref, inv_ref, east_ref, south_ref, last_ref, h_buf, u_buf, v_buf, stage, picked_ref):
    level, band = lax.axis_index("comp"), lax.axis_index("band")
    first_row, total_rows = band * ROWS, lax.axis_size("band") * ROWS
    stride = 3 * EXT

    for k in range(LEVELS):
        for f in range(3):
            rows = slice((k * 3 + f) * EXT, (k * 3 + f + 1) * EXT)
            for i in range(TILES):
                stage[i, rows, :] = fields[k, f, :, columns(i)]

    @pl.loop(0, EXT)
    def _(j):
        for f, buf in enumerate((h_buf, u_buf, v_buf)):
            buf[j] = level_rows(stage, f * EXT + j, stride)

    depth = lax.broadcasted_iota(jnp.int32, (LEVELS, NX), 0)

    def geopot(h):
        total = h
        for gap in (1, 2, 4):
            moved = pltpu.roll(total, LEVELS - gap, 0)
            total = total + jnp.where(depth < LEVELS - gap, moved, 0.0)
        return gravity * total

    def south_flux(h_a, h_b, v_a, v_b, face):
        at = first_row + face - HALO
        inside = jnp.logical_and(at > 0, at < total_rows)
        scale = jnp.where(inside, 0.25 * time_step, 0.0)
        return scale * ((v_a + v_b) * (h_a + h_b))

    for step in range(STEPS):
        reach = reach_of(step)
        low, high = HALO - reach, HALO + ROWS + reach
        for j in (low - 2, low - 1, high, high + 1):
            inv_ref[step, j] = 1.0 / jnp.maximum(h_buf[j], mass_floor)
        h_before, h_here = h_buf[low - 1], h_buf[low]
        v_before, v_here = v_buf[low - 1], v_buf[low]
        south = south_flux(h_before, h_here, v_before, v_here, low)
        south_ref[step, low] = south

        def row(j, carry, step=step):
            h, v, geo_before, geo, south = carry
            h_after, v_after, u = h_buf[j + 1], v_buf[j + 1], u_buf[j]
            geo_after = geopot(h_after)
            south_after = south_flux(h, h_after, v, v_after, j + 1)
            east = (0.25 * time_step) * ((u + roll(u, -1)) * (h + roll(h, -1)))
            inv_ref[step, j] = 1.0 / jnp.maximum(h, mass_floor)
            east_ref[step, j] = east
            south_ref[step, j + 1] = south_after
            h_buf[j] = h - ((east - roll(east, 1)) + (south_after - south))
            u_buf[j] = u + time_step * (coriolis * v - 0.5 * (roll(geo, -1) - roll(geo, 1)))
            v_buf[j] = v - time_step * (coriolis * u + 0.5 * (geo_after - geo_before))
            return h_after, v_after, geo, geo_after, south_after

        carry = (h_here, v_here, geopot(h_before), geopot(h_here), south)
        for j in range(low, high):
            carry = row(j, carry)

    own = lax.broadcasted_iota(jnp.int32, (LEVELS, NX), 0) == level
    for f, buf in enumerate((h_buf, u_buf, v_buf)):
        for j in range(ROWS):
            picked = jnp.where(own, buf[HALO + j], 0.0)
            picked_ref[pl.ds(f * ROWS + j, 1), :] = jnp.sum(picked, axis=0, keepdims=True)
    last_ref[...] = permuted(picked_ref[...], back_ref[...])


def advance_slot(limited, buf, stage, inv_ref, east_ref, south_ref):
    def face(a_out, a, b, b_out):
        raw = (7.0 / 12.0) * (a + b) - (1.0 / 12.0) * (a_out + b_out)
        bounded = jnp.maximum(jnp.minimum(raw, jnp.maximum(a, b)), jnp.minimum(a, b))
        return jnp.where(limited, bounded, raw)

    for step in range(STEPS):
        reach = reach_of(step)
        low, high = HALO - reach, HALO + ROWS + reach

        def ratios(j, n, step=step):
            return buf[j : j + n] * inv_ref[step, j : j + n]

        r = ratios(low - 2, 4)
        south = south_ref[step, low : low + 1] * face(r[0:1], r[1:2], r[2:3], r[3:4])
        r = r[1:]
        for j in range(low, high, BLOCK):
            r = jnp.concatenate([r, ratios(j + 2, BLOCK)], axis=0)
            here = r[1 : BLOCK + 1]
            after = south_ref[step, j + 1 : j + 1 + BLOCK] * face(
                r[0:BLOCK], here, r[2 : BLOCK + 2], r[3 : BLOCK + 3]
            )
            south = jnp.concatenate([south, after], axis=0)
            east = east_ref[step, j : j + BLOCK] * face(
                roll(here, 1), here, roll(here, -1), roll(here, -2)
            )
            new = buf[j : j + BLOCK] - ((east - roll(east, 1)) + (after - south[:BLOCK]))
            if step < STEPS - 1:
                buf[j : j + BLOCK] = new
            else:
                for k in range(BLOCK):
                    for i in range(TILES):
                        place = pl.ds(j + k - HALO, LEVELS, stride=ROWS)
                        stage[i, place, :] = new[k][:, columns(i)]
            r, south = r[BLOCK:], south[BLOCK:]


def kernel(
    counts_ref, flags_ref, h_ref, u_ref, v_ref, mass_ref,
    out_ref, last_ref,
    own_ref, deal_ref, back_ref, fields, masses, lows, highs, inv_ref, east_ref, south_ref,
    h_buf, u_buf, v_buf, g_stage, picked_ref, buf, dealt, stage, low_stage, high_stage,
    load_sem, rows_send, rows_recv, side_send, side_recv,
    field_send, field_recv, swap_sem, first_sem,
):
    n_comp, n_band = lax.axis_size("comp"), lax.axis_size("band")
    level, band = lax.axis_index("comp"), lax.axis_index("band")
    core = lax.rem(band, 2)
    beside = level + 1 - 2 * lax.rem(level, 2)
    sibling = band + 1 - 2 * core
    has_low, has_high = band > 0, band < n_band - 1
    outer = lax.rem(band + n_band - 1 + 2 * core, n_band)
    has_outer = jnp.logical_and(band > 0, band < n_band - 1)
    slots = masses.shape[0]

    count, start = counts_ref[level], 0
    for g in range(n_comp):
        start = start + jnp.where(g < level, counts_ref[g], 0)
    last_flag = flags_ref.shape[0] - 1

    def load(t):
        return pltpu.make_async_copy(mass_ref.at[t], masses.at[t], load_sem.at[t])

    def down(t):
        return pltpu.make_async_remote_copy(
            src_ref=mass_ref.at[t, :, pl.ds(0, HALO), :],
            dst_ref=highs.at[t],
            send_sem=rows_send.at[0, t],
            recv_sem=rows_recv.at[0, t],
            device_id={"band": lax.max(band - 1, 0)},
            device_id_type=MESH_ID,
        )

    def up(t):
        return pltpu.make_async_remote_copy(
            src_ref=mass_ref.at[t, :, pl.ds(HALO, HALO), :],
            dst_ref=lows.at[t],
            send_sem=rows_send.at[1, t],
            recv_sem=rows_recv.at[1, t],
            device_id={"band": lax.min(band + 1, n_band - 1)},
            device_id_type=MESH_ID,
        )

    def send_rows(first, last):
        @pl.loop(first, last)
        def _(t):
            @pl.when(has_low)
            def _():
                down(t).start()

            @pl.when(has_high)
            def _():
                up(t).start()

    firsts = []
    for f, ref in enumerate((h_ref, u_ref, v_ref)):
        firsts.append((ref, own_ref.at[pl.ds(f * ROWS, ROWS), :]))
    firsts = [
        pltpu.make_async_copy(src, dst, first_sem.at[n]) for n, (src, dst) in enumerate(firsts)
    ]
    for first in firsts:
        first.start()

    barrier = pltpu.get_barrier_semaphore()
    peers = [{"comp": beside}, {"band": sibling}]
    peers += [{"comp": lax.rem(level + 2 * p, n_comp)} for p in range(1, n_comp // 2)]
    for peer in peers:
        pl.semaphore_signal(barrier, inc=1, device_id=peer, device_id_type=MESH_ID)

    @pl.when(has_outer)
    def _():
        pl.semaphore_signal(barrier, inc=1, device_id={"band": outer}, device_id_type=MESH_ID)

    @pl.loop(0, slots)
    def _(t):
        load(t).start()

    make_dealing(deal_ref, False)
    for first in firsts:
        first.wait()
    own = permuted(own_ref[...], deal_ref[...])
    for f in range(3):
        fields[level, f, HALO : HALO + ROWS, :] = own[f * ROWS : (f + 1) * ROWS]

    edge = pl.multiple_of(2 * (HALO + HALO // 2) * core, HALO)

    @pl.when(jnp.logical_not(has_outer))
    def _():
        fields[level, :, pl.ds(edge, HALO), :] = jnp.zeros((3, HALO, NX), jnp.float32)

    @pl.when(jnp.logical_not(has_low))
    def _():
        lows[...] = jnp.zeros_like(lows)

    @pl.when(jnp.logical_not(has_high))
    def _():
        highs[...] = jnp.zeros_like(highs)

    pl.semaphore_wait(barrier, len(peers) + has_outer.astype(jnp.int32))

    side = pltpu.make_async_remote_copy(
        src_ref=fields.at[level, :, pl.ds(pl.multiple_of(HALO + HALO * core, HALO), HALO), :],
        dst_ref=fields.at[level, :, pl.ds(pl.multiple_of(3 * HALO * (1 - core), HALO), HALO), :],
        send_sem=side_send,
        recv_sem=side_recv,
        device_id={"band": outer},
        device_id_type=MESH_ID,
    )

    @pl.when(has_outer)
    def _():
        side.start()

    def piece(k, owner, target, lane):
        rows = pl.ds(HALO, ROWS) if k == 0 else pl.ds(edge, HALO)
        return pltpu.make_async_remote_copy(
            src_ref=fields.at[owner, :, rows, :],
            dst_ref=fields.at[owner, :, rows, :],
            send_sem=field_send.at[k, lane],
            recv_sem=field_recv.at[k, lane],
            device_id={"comp": target},
            device_id_type=MESH_ID,
        )

    ring = range(1, n_comp // 2)

    def to_all(k):
        sends = [piece(k, level, beside, 0)]
        sends += [piece(k, level, lax.rem(level + 2 * p, n_comp), p) for p in ring]
        return sends

    def passed_on(k):
        return [piece(k, beside, lax.rem(level + 2 * p, n_comp), n_comp // 2 + p) for p in ring]

    def arriving(k):
        far = [lax.rem(level + n_comp - 2 * p, n_comp) for p in ring]
        waits = [piece(k, owner, beside, p) for p, owner in zip(ring, far)]
        far = [lax.rem(beside + n_comp - 2 * p, n_comp) for p in ring]
        return waits + [piece(k, owner, beside, n_comp // 2 + p) for p, owner in zip(ring, far)]

    def deal_slots(first, last):
        @pl.loop(first, last)
        def _(t):
            load(t).wait()
            block = permuted(masses[t].reshape(LEVELS * ROWS, NX), deal_ref[...])
            for i in range(TILES):
                dealt[t, i] = block[:, columns(i)]

    ahead = AHEAD * (1 - core)
    send_rows(0, ahead)
    for send in to_all(0):
        send.start()
    make_dealing(back_ref, True)

    @pl.when(has_outer)
    def _():
        side.wait_recv()

    for send in to_all(1):
        send.start()
    for k in range(2):
        piece(k, beside, beside, 0).wait_recv()
        for send in passed_on(k):
            send.start()
    send_rows(ahead, EARLY)
    deal_slots(0, slots)
    for wait in arriving(0):
        wait.wait_recv()

    swap = pltpu.make_async_remote_copy(
        src_ref=fields.at[:, :, pl.ds(pl.multiple_of(2 * HALO - HALO * core, HALO), HALO), :],
        dst_ref=fields.at[:, :, pl.ds(pl.multiple_of(3 * HALO * core, HALO), HALO), :],
        send_sem=swap_sem.at[0],
        recv_sem=swap_sem.at[1],
        device_id={"band": sibling},
        device_id_type=MESH_ID,
    )
    swap.start()
    send_rows(EARLY, slots)
    for wait in arriving(1):
        wait.wait_recv()
    swap.wait_recv()

    dynamics(
        fields, back_ref, inv_ref, east_ref, south_ref, last_ref,
        h_buf, u_buf, v_buf, g_stage, picked_ref,
    )

    @pl.loop(0, slots)
    def _(t):
        @pl.when(has_low)
        def _():
            up(t).wait_recv()

        @pl.when(has_high)
        def _():
            down(t).wait_recv()

        sides = (LEVELS * HALO, NX)
        blocks = (
            (lows[t].reshape(sides), low_stage),
            (highs[t].reshape(sides), high_stage),
        )
        for block, to in blocks:
            moved = permuted(block, deal_ref[...])
            for i in range(TILES):
                to[i] = moved[:, columns(i)]
        for j in range(HALO):
            buf[j] = level_rows(low_stage, j, HALO)
            buf[HALO + ROWS + j] = level_rows(high_stage, j, HALO)
        for j in range(ROWS):
            buf[HALO + j] = level_rows(dealt.at[t], j, ROWS)
        limited = flags_ref[jnp.minimum(start + t, last_flag)] > 0
        advance_slot(limited, buf, stage, inv_ref, east_ref, south_ref)
        final = jnp.concatenate([stage[i] for i in range(TILES)], axis=1)
        final = permuted(final, back_ref[...])
        final = jnp.where(t < count, final, 0.0)
        out_ref[t] = final.reshape(LEVELS, ROWS, NX)

    @pl.loop(0, slots)
    def _(t):
        @pl.when(has_low)
        def _():
            down(t).wait_send()

        @pl.when(has_high)
        def _():
            up(t).wait_send()

    @pl.when(has_outer)
    def _():
        side.wait_send()

    swap.wait_send()
    for k in range(2):
        for send in to_all(k) + passed_on(k):
            send.wait_send()


def on_device(tracer_mass, layer_mass, zonal_wind, merid_wind, group_counts, limiter_flags):
    n_comp = lax.axis_size("comp")
    slots = tracer_mass.shape[0]

    f32 = jnp.float32
    vmem = pl.BlockSpec(memory_space=pltpu.VMEM)
    hbm = pl.BlockSpec(memory_space=pl.ANY)
    rows = pltpu.VMEM((STEPS, EXT, LEVELS, NX), f32)
    sides = pltpu.VMEM((slots, LEVELS, HALO, NX), f32)
    state = pltpu.VMEM((EXT, LEVELS, NX), f32)
    dma = pltpu.SemaphoreType.DMA
    out, last = pl.pallas_call(
        kernel,
        out_shape=(
            jax.ShapeDtypeStruct(tracer_mass.shape, f32),
            jax.ShapeDtypeStruct((3 * ROWS, NX), f32),
        ),
        in_specs=[pl.BlockSpec(memory_space=pltpu.SMEM)] * 2 + [hbm] * 4,
        out_specs=(vmem, vmem),
        scratch_shapes=[
            pltpu.VMEM((3 * ROWS, NX), f32),
            pltpu.VMEM((NX, NX), jnp.bfloat16),
            pltpu.VMEM((NX, NX), jnp.bfloat16),
            pltpu.VMEM((n_comp, 3, EXT, NX), f32),
            pltpu.VMEM(tracer_mass.shape, f32),
            sides,
            sides,
            rows,
            rows,
            rows,
            state,
            state,
            state,
            pltpu.VMEM((TILES, LEVELS * 3 * EXT, 128), f32),
            pltpu.VMEM((3 * ROWS, NX), f32),
            state,
            pltpu.VMEM((slots, TILES, LEVELS * ROWS, 128), f32),
            pltpu.VMEM((TILES, LEVELS * ROWS, 128), f32),
            pltpu.VMEM((TILES, LEVELS * HALO, 128), f32),
            pltpu.VMEM((TILES, LEVELS * HALO, 128), f32),
            dma((slots,)),
            dma((2, slots)),
            dma((2, slots)),
            dma,
            dma,
            dma((2, n_comp)),
            dma((2, n_comp)),
            dma((2,)),
            dma((3,)),
        ],
        compiler_params=pltpu.CompilerParams(
            collective_id=0, has_side_effects=True, vmem_limit_bytes=VMEM_LIMIT
        ),
    )(
        group_counts,
        limiter_flags,
        layer_mass.reshape(ROWS, NX),
        zonal_wind.reshape(ROWS, NX),
        merid_wind.reshape(ROWS, NX),
        tracer_mass,
    )
    last = last.reshape(3, 1, ROWS, NX)
    return out, last[0], last[1], last[2]


def solution(mesh):
    placed = (
        P("comp", None, "band", None),
        P("comp", "band", None),
        P("comp", "band", None),
        P("comp", "band", None),
        P(),
        P(),
    )
    return jax.shard_map(
        on_device,
        mesh=mesh,
        in_specs=placed,
        out_specs=placed[:4],
        check_vma=False,
    )
```
